32 devices in a mesh: groups: 2 (over y), role: 4 (over x, core), tp: 4 (over z).
Axes of the slice: x: 2, y: 2, z: 4, core: 2. Of those that a mesh axis runs over, the one named last changes fastest.
Arguments:
- x_teacher: bfloat16 [512, 8192], P('groups', 'tp'), parts along dimension 0, may hold values from -6 to 6
- x_student: bfloat16 [512, 4096], P('groups', 'role'), parts along dimension 0, may hold values from -6 to 6
- t_gate: bfloat16 [8192, 14336], P('tp', 'role'), may hold values from -0.0625 to 0.0625
- t_up: bfloat16 [8192, 14336], P('tp', 'role'), may hold values from -0.0625 to 0.0625
- t_down: bfloat16 [14336, 8192], P('role', 'tp'), may hold values from -0.046875 to 0.046875
- s_gate: bfloat16 [4096, 8192], P('role', 'tp'), may hold values from -0.09375 to 0.09375
- s_up: bfloat16 [4096, 8192], P('role', 'tp'), may hold values from -0.09375 to 0.09375
- s_down: bfloat16 [8192, 4096], P('tp', 'role'), may hold values from -0.0625 to 0.0625
- align: bfloat16 [4096, 8192], P('role', 'tp'), may hold values from -0.09375 to 0.09375
Outputs:
- grad_s_gate: bfloat16 [8192, 8192], P(('groups', 'role'), 'tp'), parts along dimension 0
- grad_s_up: bfloat16 [8192, 8192], P(('groups', 'role'), 'tp'), parts along dimension 0
- grad_s_down: bfloat16 [16384, 4096], P(('groups', 'tp'), 'role'), parts along dimension 0
- grad_align: bfloat16 [8192, 8192], P(('groups', 'role'), 'tp'), parts along dimension 0
The draws below stay inside these ranges and needn't reach their ends.
There are 2 independent parts, one for each index of `groups`. The reference program is written for one: setup_inputs(seed, part) draws one part's arguments, and reference() takes and returns one part's arrays. A program takes and returns all parts, laid end to end along the dimension named above; an argument that names none is the same for every part. Nothing has to cross between parts.
All inputs are finite; a program needn't handle non-finite values.
Results may differ from the reference program's by a relative error of at most 0.009.
Values may be sent and summed in bfloat16 or wider, within the bound.
A program may use at most 128 MiB of HBM per device.

```python
import jax
import jax.numpy as jnp
from jax import lax

DT = 8192
DS = 4096
FT = 14336
FS = 8192
TOK = 256


def strengthened(values, stream_key, source, target, blocks, factor):
    def block_of(position):
        return (jnp.arange(values.shape[position]) // (values.shape[position] // blocks)).reshape((-1,) + (1,) * (values.ndim - 1 - position))

    first = jax.random.permutation(stream_key, blocks)[block_of(target)]
    other_side = (block_of(target) + blocks // 2) % blocks
    return jnp.where((block_of(source) == first) | (block_of(source) == other_side), factor * values, values)


def steps_of(stream_key, dims, split, low, high):
    gain = 1.0
    for axis_at, parts in split:
        draws = jax.random.uniform(jax.random.fold_in(jax.random.fold_in(stream_key, 6), axis_at), (parts,), jnp.float32, low / len(split), high / len(split))
        gain = gain * jnp.repeat(jnp.exp(draws), dims[axis_at] // parts).reshape((-1,) + (1,) * (len(dims) - 1 - axis_at))
    return gain


def gaussian(key, dims, scale, bound, shards=(), dtype=jnp.bfloat16):
    drawn = jax.random.normal(key, dims, jnp.float32) * scale
    if len(shards) > 0:
        drawn = steps_of(key, dims, shards, -0.22, 0.18) * drawn
    return jnp.clip(drawn, min=-bound, max=bound).astype(dtype)


def bell_draw_with(key, shape, spread, limit, shards, heavy, dtype=jnp.bfloat16):
    result = spread * jax.random.normal(key, shape, jnp.float32)
    if shards:
        result = result * steps_of(key, shape, shards, -0.22, 0.18)
    return jnp.clip(strengthened(result, jax.random.fold_in(key, 3), *heavy), -limit, limit).astype(dtype)


def setup_inputs(seed: int = 0, part: int = 0) -> dict:
    seeds = jax.random.split(jax.random.key(seed), 10)
    part_splits = jax.random.split(jax.random.fold_in(seeds[9], part), 10)
    x_teacher = bell_draw_with(part_splits[0], (TOK, DT), 1.0, 6.0, ((1, 4),), (1, 0, 4, 2.0))
    x_student = gaussian(part_splits[1], (TOK, DS), 1.0, 6.0, ((1, 4),))
    t_gate = gaussian(seeds[2], (DT, FT), DT ** -0.5, 0.0625, ((0, 4), (1, 4)))
    t_up = gaussian(seeds[3], (DT, FT), DT ** -0.5, 0.0625, ((0, 4), (1, 4)))
    t_down = gaussian(seeds[4], (FT, DT), FT ** -0.5, 0.046875, ((0, 4), (1, 4)))
    s_gate = gaussian(seeds[5], (DS, FS), DS ** -0.5, 0.09375, ((0, 4), (1, 4)))
    s_up = gaussian(seeds[6], (DS, FS), DS ** -0.5, 0.09375, ((0, 4), (1, 4)))
    s_down = gaussian(seeds[7], (FS, DS), FS ** -0.5, 0.0625, ((0, 4), (1, 4)))
    align = gaussian(seeds[8], (DS, DT), DS ** -0.5, 0.09375, ((0, 4), (1, 4)))
    return dict(x_teacher=x_teacher, x_student=x_student, t_gate=t_gate, t_up=t_up, t_down=t_down, s_gate=s_gate, s_up=s_up, s_down=s_down, align=align)


loss_scale = 16.0


def contract_rows(left, right):
    return lax.dot_general(left, right, (((0,), (0,)), ((), ())), preferred_element_type=jnp.float32)


def contract_cols(left, right):
    return lax.dot_general(left, right, (((1,), (1,)), ((), ())), preferred_element_type=jnp.float32)


def reference(x_teacher, x_student, t_gate, t_up, t_down, s_gate, s_up, s_down, align):
    teacher_gate = jnp.dot(x_teacher, t_gate, preferred_element_type=jnp.float32)
    teacher_up = jnp.dot(x_teacher, t_up, preferred_element_type=jnp.float32)
    teacher_hidden = (jax.nn.silu(teacher_gate) * teacher_up).astype(jnp.bfloat16)
    features = jnp.dot(teacher_hidden, t_down, preferred_element_type=jnp.float32)
    student_gate = jnp.dot(x_student, s_gate, preferred_element_type=jnp.float32)
    student_up = jnp.dot(x_student, s_up, preferred_element_type=jnp.float32)
    gate_sigmoid = jax.nn.sigmoid(student_gate)
    gate_active = student_gate * gate_sigmoid
    student_hidden = (gate_active * student_up).astype(jnp.bfloat16)
    student_out = jnp.dot(student_hidden, s_down, preferred_element_type=jnp.float32).astype(jnp.bfloat16)
    aligned = jnp.dot(student_out, align, preferred_element_type=jnp.float32)
    grad_aligned = ((aligned - features) * (2.0 * loss_scale / TOK)).astype(jnp.bfloat16)
    grad_align = contract_rows(student_out, grad_aligned).astype(jnp.bfloat16)
    grad_student_out = contract_cols(grad_aligned, align).astype(jnp.bfloat16)
    grad_s_down = contract_rows(student_hidden, grad_student_out).astype(jnp.bfloat16)
    grad_hidden = contract_cols(grad_student_out, s_down)
    slope = gate_sigmoid * (1.0 + student_gate * (1.0 - gate_sigmoid))
    grad_gate_pre = (grad_hidden * student_up * slope).astype(jnp.bfloat16)
    grad_up_pre = (grad_hidden * gate_active).astype(jnp.bfloat16)
    grad_s_gate = contract_rows(x_student, grad_gate_pre).astype(jnp.bfloat16)
    grad_s_up = contract_rows(x_student, grad_up_pre).astype(jnp.bfloat16)
    return (grad_s_gate, grad_s_up, grad_s_down, grad_align)
```

```python
import functools

import jax
import jax.numpy as jnp
from jax import lax
from jax.experimental import pallas as pl
from jax.experimental.pallas import tpu as pltpu
from jax.sharding import PartitionSpec as P

loss_scale = 16.0
MESH = pl.DeviceIdType.MESH
BF16 = jnp.bfloat16
F32 = jnp.float32
SKEW = 2
TEACHER_SLOTS = 3
DOWN_SLOTS = 3
PIECES = 4


def width_of(columns, wanted):
    width = wanted
    while columns % width:
        width //= 2
    return width


def sum_scratch(devices, half, columns, first_type, finals):
    peers = devices // 2 - 1
    return dict(
        sent1=pltpu.VMEM((half, columns), first_type),
        got1=pltpu.VMEM((half, columns), first_type),
        sent2=pltpu.VMEM((half, columns), BF16),
        got2=pltpu.VMEM((peers, half, columns), BF16),
        s1=pltpu.SemaphoreType.DMA((PIECES,)),
        r1=pltpu.SemaphoreType.DMA((PIECES,)),
        s2=pltpu.SemaphoreType.DMA((peers, PIECES)),
        r2=pltpu.SemaphoreType.DMA((peers, PIECES)),
        s3=pltpu.SemaphoreType.DMA((finals, PIECES)),
        r3=pltpu.SemaphoreType.DMA((finals, PIECES)),
    )


class Summed:
    def __init__(self, axis, part, columns, bufs, finals, finish):
        self.axis = axis
        self.count = lax.axis_size(axis)
        self.me = lax.axis_index(axis)
        self.own = lax.rem(self.me, 2)
        self.pair = self.me + 1 - 2 * self.own
        self.part, self.columns, self.b = part, columns, bufs
        self.finals, self.finish = finals, finish
        self.half = part.shape[1]
        self.step = self.half // PIECES
        self.tile = width_of(columns, 1024)

    def rows(self, k):
        return pl.ds(k * self.step, self.step)

    def tiles(self):
        return [pl.ds(j, self.tile) for j in range(0, self.columns, self.tile)]

    def copy1(self, k):
        rows = self.rows(k)
        return pltpu.make_async_remote_copy(
            src_ref=self.b["sent1"].at[rows], dst_ref=self.b["got1"].at[rows],
            send_sem=self.b["s1"].at[k], recv_sem=self.b["r1"].at[k],
            device_id={self.axis: self.pair}, device_id_type=MESH)

    def copy2(self, j, k):
        rows = self.rows(k)
        return pltpu.make_async_remote_copy(
            src_ref=self.b["sent2"].at[rows], dst_ref=self.b["got2"].at[j, rows],
            send_sem=self.b["s2"].at[j, k], recv_sem=self.b["r2"].at[j, k],
            device_id={self.axis: lax.rem(self.me + 2 * (j + 1), self.count)},
            device_id_type=MESH)

    def copy3(self, i, k, owner):
        rows = self.rows(k)
        ref = self.finals[i].at[owner, rows]
        return pltpu.make_async_remote_copy(
            src_ref=ref, dst_ref=ref,
            send_sem=self.b["s3"].at[i, k], recv_sem=self.b["r3"].at[i, k],
            device_id={self.axis: self.pair}, device_id_type=MESH)

    def phase1(self):
        for k in range(PIECES):
            rows = self.rows(k)
            for cols in self.tiles():
                self.b["sent1"][rows, cols] = self.part[1 - self.own, rows, cols].astype(
                    self.b["sent1"].dtype)
            self.copy1(k).start()

    def phase2(self):
        for k in range(PIECES):
            rows = self.rows(k)
            self.copy1(k).wait_recv()
            for cols in self.tiles():
                total = self.part[self.own, rows, cols] + self.b["got1"][rows, cols].astype(F32)
                self.part[self.own, rows, cols] = total
                self.b["sent2"][rows, cols] = total.astype(BF16)
            for j in range(self.count // 2 - 1):
                self.copy2(j, k).start()

    def phase3(self):
        for k in range(PIECES):
            rows = self.rows(k)
            for j in range(self.count // 2 - 1):
                self.copy2(j, k).wait_recv()
            for cols in self.tiles():
                total = self.part[self.own, rows, cols]
                for j in range(self.count // 2 - 1):
                    total = total + self.b["got2"][j, rows, cols].astype(F32)
                self.part[self.own, rows, cols] = total
            self.finish(self.own, rows)
            for i in range(len(self.finals)):
                self.copy3(i, k, self.own).start()

    def phase4(self):
        for k in range(PIECES):
            for i in range(len(self.finals)):
                self.copy3(i, k, 1 - self.own).wait_recv()

    def drain(self):
        for k in range(PIECES):
            self.copy1(k).wait_send()
            for j in range(self.count // 2 - 1):
                self.copy2(j, k).wait_send()
            for i in range(len(self.finals)):
                self.copy3(i, k, self.own).wait_send()


def whole(ref):
    return ref[...].reshape(ref.shape[0] * ref.shape[1], ref.shape[2])


def exchange_kernel(names, chunk, x_t, x_s, tg, tu, td, sg, su, sd, al,
                    o_so, o_ga, o_sh, o_gso, o_gg, o_gu, *scratch):
    s = jax.tree.unflatten(names, scratch)
    tp, role = lax.axis_size("tp"), lax.axis_size("role")
    me, my_role = lax.axis_index("tp"), lax.axis_index("role")
    tokens = x_t.shape[0]
    half = tokens // 2
    units = tg.shape[1]
    chunks = units // chunk
    student_units = sg.shape[1]
    held = s["sums"].shape[0]
    last = tp - 1

    def teacher_load(c):
        cols = pl.ds(pl.multiple_of(c * chunk, chunk), chunk)
        slot = lax.rem(c, TEACHER_SLOTS)
        return (
            pltpu.make_async_copy(tg.at[:, cols], s["t_slot"].at[slot, 0], s["t_sem"].at[slot, 0]),
            pltpu.make_async_copy(tu.at[:, cols], s["t_slot"].at[slot, 1], s["t_sem"].at[slot, 1]),
        )

    def down_load(c):
        slot = lax.rem(c, DOWN_SLOTS)
        return pltpu.make_async_copy(
            td.at[pl.ds(pl.multiple_of(c * chunk, chunk), chunk)],
            s["d_slot"].at[slot], s["d_sem"].at[slot])

    load_sg = pltpu.make_async_copy(sg, s["w_gate"], s["w_sem"].at[0])
    load_su = pltpu.make_async_copy(su, s["w_gate"], s["w_sem"].at[1])
    load_sd = pltpu.make_async_copy(sd, s["w_down"], s["w_sem"].at[2])
    load_al = pltpu.make_async_copy(al, s["w_align"], s["w_sem"].at[3])

    for c in range(min(TEACHER_SLOTS, chunks)):
        for load in teacher_load(c):
            load.start()
    load_sg.start()
    load_sd.start()
    load_al.start()
    for c in range(min(DOWN_SLOTS, chunks)):
        down_load(c).start()

    barrier = pltpu.get_barrier_semaphore()
    for other in range(1, tp):
        pl.semaphore_signal(barrier, inc=1, device_id={"tp": lax.rem(me + other, tp)},
                            device_id_type=MESH)
    for other in range(1, role):
        pl.semaphore_signal(barrier, inc=1, device_id={"role": lax.rem(my_role + other, role)},
                            device_id_type=MESH)
    pl.semaphore_wait(barrier, tp + role - 2)

    s["diff"][...] = jnp.zeros_like(s["diff"])

    def rs_copy(way, c, target):
        ref = s["run"].at[way, c]
        return pltpu.make_async_remote_copy(
            src_ref=ref, dst_ref=ref, send_sem=s["run_s"].at[way, c],
            recv_sem=s["run_r"].at[way, c], device_id={"tp": target}, device_id_type=MESH)

    def ag_copy(way, c, target):
        ref = s["hid"].at[c, way]
        return pltpu.make_async_remote_copy(
            src_ref=ref, dst_ref=ref, send_sem=s["hid_s"].at[way, c],
            recv_sem=s["hid_r"].at[way, c], device_id={"tp": target}, device_id_type=MESH)

    def finish_hidden(own, rows):
        tile = width_of(student_units, 1024)
        for j in range(0, student_units, tile):
            gate = s["gate_up"][own, rows, pl.ds(j, tile)]
            up = s["gate_up"][own, rows, pl.ds(student_units + j, tile)]
            s["sh"][own, rows, pl.ds(j, tile)] = (gate * jax.nn.sigmoid(gate) * up).astype(BF16)

    def finish_out(own, rows):
        s["so"][own, rows] = s["narrow"][own, rows].astype(BF16)

    def finish_diff(own, rows):
        s["ga"][own, rows] = (s["diff"][own, rows] * (2.0 * loss_scale / tokens)).astype(BF16)

    def finish_grad_out(own, rows):
        s["gso"][own, rows] = s["narrow"][own, rows].astype(BF16)

    def finish_grad_hidden(own, rows):
        tile = width_of(student_units, 1024)
        for j in range(0, student_units, tile):
            gate = s["gate_up"][own, rows, pl.ds(j, tile)]
            up = s["gate_up"][own, rows, pl.ds(student_units + j, tile)]
            grad = s["diff"][own, rows, pl.ds(j, tile)]
            sigmoid = jax.nn.sigmoid(gate)
            slope = sigmoid * (1.0 + gate * (1.0 - sigmoid))
            s["gg"][own, rows, pl.ds(j, tile)] = (grad * up * slope).astype(BF16)
            s["gu"][own, rows, pl.ds(j, tile)] = (grad * (gate * sigmoid)).astype(BF16)

    wide, narrow = sg.shape[1], sd.shape[1]
    sum_gate = Summed("role", s["gate_up"], 2 * student_units, s["b_gate"], [s["sh"]], finish_hidden)
    sum_out = Summed("tp", s["narrow"], narrow, s["b_out"], [s["so"]], finish_out)
    sum_diff = Summed("role", s["diff"], al.shape[1], s["b_diff"], [s["ga"]], finish_diff)
    sum_grad = Summed("tp", s["narrow"], narrow, s["b_grad"], [s["gso"]], finish_grad_out)
    sum_hidden = Summed("role", s["diff"], wide, s["b_hidden"], [s["gg"], s["gu"]],
                        finish_grad_hidden)

    def product(left, right, out, first_col, columns, transposed, add):
        tile = width_of(columns, 256)

        @pl.loop(0, columns // tile)
        def _(j):
            at = pl.multiple_of(j * tile, tile)
            if transposed:
                block = lax.dot_general(left, right[pl.ds(at, tile)], (((1,), (1,)), ((), ())),
                                        preferred_element_type=F32)
            else:
                block = jnp.dot(left, right[:, pl.ds(at, tile)], preferred_element_type=F32)
            block = block.reshape(2, half, tile)
            cols = pl.ds(pl.multiple_of(first_col + at, tile), tile)
            if add:
                out[:, :, cols] = out[:, :, cols] + block
            else:
                out[:, :, cols] = block

    def student_gate():
        load_sg.wait()
        product(x_s[...], s["w_gate"], s["gate_up"], 0, student_units, False, False)
        load_su.start()

    def student_up():
        load_su.wait()
        product(x_s[...], s["w_gate"], s["gate_up"], student_units, student_units, False, False)
        sum_gate.phase1()

    def student_down():
        sum_gate.phase4()
        load_sd.wait()
        product(whole(s["sh"]), s["w_down"], s["narrow"], 0, narrow, False, False)
        sum_out.phase1()

    def student_align():
        sum_out.phase4()
        load_al.wait()
        product(whole(s["so"]), s["w_align"], s["diff"], 0, al.shape[1], False, True)

    steps = max(chunks + 2 * SKEW * last, 18)
    plan = [student_gate, student_up, sum_gate.phase2, sum_gate.phase3, student_down,
            sum_out.phase2, sum_out.phase3, student_align]
    wanted = [1, 2, 3, 9, 10, 12, 15, 17]

    @pl.loop(0, steps)
    def _(t):
        @pl.when(t < chunks)
        def _():
            for load in teacher_load(t):
                load.wait()
            slot = lax.rem(t, TEACHER_SLOTS)
            for k in range(2):
                block = jnp.dot(x_t[...], s["t_slot"][slot, k], preferred_element_type=F32)
                s["sums"][lax.rem(t, held), :, :, k * chunk:(k + 1) * chunk] = block.reshape(
                    2, half, chunk)

            @pl.when(t + TEACHER_SLOTS < chunks)
            def _():
                for load in teacher_load(t + TEACHER_SLOTS):
                    load.start()

        for way in range(2):
            hop = last - me if way == 0 else me
            onward = lax.rem(me + (tp - 1 if way == 0 else 1), tp)
            back = lax.rem(me + (1 if way == 0 else tp - 1), tp)
            c = t - SKEW * hop

            @pl.when((c >= 0) & (c < chunks))
            def _():
                at = lax.rem(c, held)

                @pl.when(hop == 0)
                def _():
                    s["run"][way, c] = s["sums"][at, way].astype(BF16)
                    rs_copy(way, c, onward).start()

                @pl.when((hop > 0) & (hop < last))
                def _():
                    rs_copy(way, c, onward).wait_recv()
                    s["run"][way, c] = (
                        s["sums"][at, way] + s["run"][way, c].astype(F32)).astype(BF16)
                    rs_copy(way, c, onward).start()

                @pl.when(hop == last)
                def _():
                    rs_copy(way, c, back).wait_recv()
                    gate = s["sums"][at, way, :, :chunk] + s["run"][way, c, :, :chunk].astype(F32)
                    up = s["sums"][at, way, :, chunk:] + s["run"][way, c, :, chunk:].astype(F32)
                    s["hid"][c, way] = (gate * jax.nn.sigmoid(gate) * up).astype(BF16)
                    ag_copy(way, c, back).start()

            g = t - SKEW * last - SKEW * (last - hop)

            @pl.when((g >= 0) & (g < chunks) & (hop < last))
            def _():
                ag_copy(way, g, onward).wait_recv()

                @pl.when(hop > 0)
                def _():
                    ag_copy(way, g, back).start()

        f = t - 2 * SKEW * last

        @pl.when((f >= 0) & (f < chunks))
        def _():
            down_load(f).wait()
            left = s["hid"][f].reshape(tokens, chunk)
            slot = lax.rem(f, DOWN_SLOTS)
            wide_tile = width_of(td.shape[1], 512)

            @pl.loop(0, td.shape[1] // wide_tile)
            def _(j):
                cols = pl.ds(pl.multiple_of(j * wide_tile, wide_tile), wide_tile)
                block = jnp.dot(left, s["d_slot"][slot, :, cols], preferred_element_type=F32)
                s["diff"][:, :, cols] = s["diff"][:, :, cols] - block.reshape(2, half, wide_tile)

            @pl.when(f + DOWN_SLOTS < chunks)
            def _():
                down_load(f + DOWN_SLOTS).start()

        for at, work in zip(wanted, plan):
            pl.when(t == at)(work)

    sum_diff.phase1()
    sum_diff.phase2()
    sum_diff.phase3()
    sum_diff.phase4()
    sum_out.drain()
    product(whole(s["ga"]), s["w_align"], s["narrow"], 0, narrow, True, False)
    sum_grad.phase1()
    sum_grad.phase2()
    sum_grad.phase3()
    sum_grad.phase4()
    sum_diff.drain()
    product(whole(s["gso"]), s["w_down"], s["diff"], 0, wide, True, False)
    sum_hidden.phase1()
    sum_hidden.phase2()

    stores = [
        pltpu.make_async_copy(s[name], out, s["o_sem"].at[i])
        for i, (name, out) in enumerate(
            [("so", o_so), ("ga", o_ga), ("sh", o_sh), ("gso", o_gso), ("gg", o_gg), ("gu", o_gu)])
    ]
    for store in stores[:4]:
        store.start()
    sum_hidden.phase3()
    sum_hidden.phase4()
    for store in stores[4:]:
        store.start()
    sum_gate.drain()
    sum_grad.drain()
    sum_hidden.drain()

    @pl.loop(0, chunks)
    def _(c):
        for way in range(2):
            hop = last - me if way == 0 else me
            onward = lax.rem(me + (tp - 1 if way == 0 else 1), tp)
            back = lax.rem(me + (1 if way == 0 else tp - 1), tp)

            @pl.when(hop < last)
            def _():
                rs_copy(way, c, onward).wait_send()

            @pl.when(hop > 0)
            def _():
                ag_copy(way, c, back).wait_send()

    for store in stores:
        store.wait()


def exchanged(x_teacher, x_student, t_gate, t_up, t_down, s_gate, s_up, s_down, align):
    tp, role = lax.axis_size("tp"), lax.axis_size("role")
    tokens, depth = x_teacher.shape
    half = tokens // 2
    units = t_gate.shape[1]
    chunk = width_of(units, 256)
    chunks = units // chunk
    wide, narrow, features = s_gate.shape[1], s_down.shape[1], align.shape[1]
    DMA = pltpu.SemaphoreType.DMA
    scratch = dict(
        sums=pltpu.VMEM((min(chunks, SKEW * (tp - 1) + 1), 2, half, 2 * chunk), F32),
        run=pltpu.VMEM((2, chunks, half, 2 * chunk), BF16),
        run_s=DMA((2, chunks)), run_r=DMA((2, chunks)),
        hid=pltpu.VMEM((chunks, 2, half, chunk), BF16),
        hid_s=DMA((2, chunks)), hid_r=DMA((2, chunks)),
        t_slot=pltpu.VMEM((TEACHER_SLOTS, 2, depth, chunk), BF16),
        t_sem=DMA((TEACHER_SLOTS, 2)),
        d_slot=pltpu.VMEM((DOWN_SLOTS, chunk, features), BF16),
        d_sem=DMA((DOWN_SLOTS,)),
        w_gate=pltpu.VMEM(s_gate.shape, BF16),
        w_down=pltpu.VMEM(s_down.shape, BF16),
        w_align=pltpu.VMEM(align.shape, BF16),
        w_sem=DMA((4,)),
        gate_up=pltpu.VMEM((2, half, 2 * wide), F32),
        narrow=pltpu.VMEM((2, half, narrow), F32),
        diff=pltpu.VMEM((2, half, max(features, wide)), F32),
        so=pltpu.VMEM((2, half, narrow), BF16),
        ga=pltpu.VMEM((2, half, features), BF16),
        sh=pltpu.VMEM((2, half, wide), BF16),
        gso=pltpu.VMEM((2, half, narrow), BF16),
        gg=pltpu.VMEM((2, half, wide), BF16),
        gu=pltpu.VMEM((2, half, wide), BF16),
        o_sem=DMA((6,)),
        b_gate=sum_scratch(role, half, 2 * wide, BF16, 1),
        b_out=sum_scratch(tp, half, narrow, BF16, 1),
        b_diff=sum_scratch(role, half, features, BF16, 1),
        b_grad=sum_scratch(tp, half, narrow, BF16, 1),
        b_hidden=sum_scratch(role, half, wide, BF16, 2),
    )
    leaves, names = jax.tree.flatten(scratch, is_leaf=lambda leaf: not isinstance(leaf, dict))
    shapes = [narrow, features, wide, narrow, wide, wide]
    outs = pl.pallas_call(
        functools.partial(exchange_kernel, names, chunk),
        out_shape=[jax.ShapeDtypeStruct((2, half, n), BF16) for n in shapes],
        in_specs=[pl.BlockSpec(memory_space=pltpu.VMEM)] * 2 + [pl.BlockSpec(memory_space=pl.ANY)] * 7,
        out_specs=[pl.BlockSpec(memory_space=pl.ANY)] * 6,
        scratch_shapes=leaves,
        compiler_params=pltpu.CompilerParams(
            collective_id=0, has_side_effects=True, vmem_limit_bytes=60 * 2**20),
        cost_estimate=pl.CostEstimate(flops=20 * 10**9, bytes_accessed=70 * 10**6, transcendentals=10**6),
    )(x_teacher, x_student, t_gate, t_up, t_down, s_gate, s_up, s_down, align)
    return [out.reshape(tokens, out.shape[2]) for out in outs]


def outer_kernel(*refs):
    count = len(refs) // 3
    for i in range(count):
        refs[2 * count + i][...] = lax.dot_general(
            refs[i][...], refs[count + i][...], (((0,), (0,)), ((), ())),
            preferred_element_type=F32).astype(BF16)


def outer_products(lefts, rights):
    tokens = lefts[0].shape[0]
    steps = min(8, min(left.shape[1] for left in lefts) // 128)
    in_specs = [pl.BlockSpec((tokens, left.shape[1] // steps), lambda i: (0, i)) for left in lefts]
    in_specs += [pl.BlockSpec(right.shape, lambda i: (0, 0)) for right in rights]
    return pl.pallas_call(
        outer_kernel,
        grid=(steps,),
        out_shape=[jax.ShapeDtypeStruct((left.shape[1], right.shape[1]), BF16)
                   for left, right in zip(lefts, rights)],
        in_specs=in_specs,
        out_specs=[pl.BlockSpec((left.shape[1] // steps, right.shape[1]), lambda i: (i, 0))
                   for left, right in zip(lefts, rights)],
        compiler_params=pltpu.CompilerParams(vmem_limit_bytes=48 * 2**20),
    )(*lefts, *rights)


def on_device(x_teacher, x_student, *weights):
    student_out, grad_aligned, student_hidden, grad_student_out, grad_gate_pre, grad_up_pre = exchanged(
        x_teacher, x_student, *weights)
    return tuple(outer_products(
        [x_student, x_student, student_hidden, student_out],
        [grad_gate_pre, grad_up_pre, grad_student_out, grad_aligned]))


def solution(mesh):
    placed = (
        P("groups", "tp"),
        P("groups", "role"),
        P("tp", "role"),
        P("tp", "role"),
        P("role", "tp"),
        P("role", "tp"),
        P("role", "tp"),
        P("tp", "role"),
        P("role", "tp"),
    )
    return jax.shard_map(
        on_device,
        mesh=mesh,
        in_specs=placed,
        out_specs=(
            P(("groups", "role"), "tp"),
            P(("groups", "role"), "tp"),
            P(("groups", "tp"), "role"),
            P(("groups", "role"), "tp"),
        ),
        check_vma=False,
    )
```

```python
import functools

import jax
import jax.numpy as jnp
from jax import lax
from jax.experimental import pallas as pl
from jax.experimental.pallas import tpu as pltpu
from jax.sharding import PartitionSpec as P

loss_scale = 16.0
MESH = pl.DeviceIdType.MESH
BF16 = jnp.bfloat16
F32 = jnp.float32
SKEW = 3
GROUPS = 2
TEACHER_SLOTS = 3
DOWN_SLOTS = 3
PIECES = 4


def width_of(columns, wanted):
    width = wanted
    while columns % width:
        width //= 2
    return width


def sum_scratch(devices, half, columns, first_type, finals):
    peers = devices // 2 - 1
    return dict(
        sent1=pltpu.VMEM((half, columns), first_type),
        got1=pltpu.VMEM((half, columns), first_type),
        sent2=pltpu.VMEM((half, columns), BF16),
        got2=pltpu.VMEM((peers, half, columns), BF16),
        s1=pltpu.SemaphoreType.DMA((PIECES,)),
        r1=pltpu.SemaphoreType.DMA((PIECES,)),
        s2=pltpu.SemaphoreType.DMA((peers, PIECES)),
        r2=pltpu.SemaphoreType.DMA((peers, PIECES)),
        s3=pltpu.SemaphoreType.DMA((finals, PIECES)),
        r3=pltpu.SemaphoreType.DMA((finals, PIECES)),
    )


class Summed:
    def __init__(self, axis, part, columns, bufs, finals, finish):
        self.axis = axis
        self.count = lax.axis_size(axis)
        self.me = lax.axis_index(axis)
        self.own = lax.rem(self.me, 2)
        self.pair = self.me + 1 - 2 * self.own
        self.part, self.columns, self.b = part, columns, bufs
        self.finals, self.finish = finals, finish
        self.half = part.shape[1]
        self.step = self.half // PIECES
        self.tile = width_of(columns, 1024)

    def rows(self, k):
        return pl.ds(k * self.step, self.step)

    def tiles(self):
        return [pl.ds(j, self.tile) for j in range(0, self.columns, self.tile)]

    def copy1(self, k):
        rows = self.rows(k)
        return pltpu.make_async_remote_copy(
            src_ref=self.b["sent1"].at[rows], dst_ref=self.b["got1"].at[rows],
            send_sem=self.b["s1"].at[k], recv_sem=self.b["r1"].at[k],
            device_id={self.axis: self.pair}, device_id_type=MESH)

    def copy2(self, j, k):
        rows = self.rows(k)
        return pltpu.make_async_remote_copy(
            src_ref=self.b["sent2"].at[rows], dst_ref=self.b["got2"].at[j, rows],
            send_sem=self.b["s2"].at[j, k], recv_sem=self.b["r2"].at[j, k],
            device_id={self.axis: lax.rem(self.me + 2 * (j + 1), self.count)},
            device_id_type=MESH)

    def copy3(self, i, k, owner):
        rows = self.rows(k)
        ref = self.finals[i].at[owner, rows]
        return pltpu.make_async_remote_copy(
            src_ref=ref, dst_ref=ref,
            send_sem=self.b["s3"].at[i, k], recv_sem=self.b["r3"].at[i, k],
            device_id={self.axis: self.pair}, device_id_type=MESH)

    def phase1(self, pieces=range(PIECES)):
        for k in pieces:
            rows = self.rows(k)
            for cols in self.tiles():
                self.b["sent1"][rows, cols] = self.part[1 - self.own, rows, cols].astype(
                    self.b["sent1"].dtype)
            self.copy1(k).start()

    def phase2(self, pieces=range(PIECES)):
        for k in pieces:
            rows = self.rows(k)
            self.copy1(k).wait_recv()
            for cols in self.tiles():
                total = self.part[self.own, rows, cols] + self.b["got1"][rows, cols].astype(F32)
                self.part[self.own, rows, cols] = total
                self.b["sent2"][rows, cols] = total.astype(BF16)
            for j in range(self.count // 2 - 1):
                self.copy2(j, k).start()

    def phase3(self, pieces=range(PIECES)):
        for k in pieces:
            rows = self.rows(k)
            for j in range(self.count // 2 - 1):
                self.copy2(j, k).wait_recv()
            for cols in self.tiles():
                total = self.part[self.own, rows, cols]
                for j in range(self.count // 2 - 1):
                    total = total + self.b["got2"][j, rows, cols].astype(F32)
                self.part[self.own, rows, cols] = total
            self.finish(self.own, rows)
            for i in range(len(self.finals)):
                self.copy3(i, k, self.own).start()

    def phase4(self, pieces=range(PIECES)):
        for k in pieces:
            for i in range(len(self.finals)):
                self.copy3(i, k, 1 - self.own).wait_recv()

    def drain(self):
        for k in range(PIECES):
            self.copy1(k).wait_send()
            for j in range(self.count // 2 - 1):
                self.copy2(j, k).wait_send()
            for i in range(len(self.finals)):
                self.copy3(i, k, self.own).wait_send()


def taken(ref, rows):
    block = ref[:, rows]
    return block.reshape(block.shape[0] * block.shape[1], block.shape[2])


def exchange_kernel(names, chunk, x_t, x_s, tg, tu, td, sg, su, sd, al,
                    o_so, o_ga, o_sh, o_gso, o_gg, o_gu, *scratch):
    s = jax.tree.unflatten(names, scratch)
    tp, role = lax.axis_size("tp"), lax.axis_size("role")
    me, my_role = lax.axis_index("tp"), lax.axis_index("role")
    tokens = x_t.shape[0]
    half = tokens // 2
    units = tg.shape[1]
    chunks = units // chunk
    student_units = sg.shape[1]
    last = tp - 1
    share = half // GROUPS
    items = GROUPS * chunks
    every = pl.ds(0, half)
    of_group = [pl.ds(g * share, share) for g in range(GROUPS)]
    per_group = PIECES // GROUPS
    pieces = [range(g * per_group, (g + 1) * per_group) for g in range(GROUPS)]

    def teacher_load(c):
        cols = pl.ds(pl.multiple_of(c * chunk, chunk), chunk)
        slot = lax.rem(c, TEACHER_SLOTS)
        return (
            pltpu.make_async_copy(tg.at[:, cols], s["t_slot"].at[slot, 0], s["t_sem"].at[slot, 0]),
            pltpu.make_async_copy(tu.at[:, cols], s["t_slot"].at[slot, 1], s["t_sem"].at[slot, 1]),
        )

    def down_load(i):
        slot = lax.rem(i, DOWN_SLOTS)
        first = pl.multiple_of(lax.rem(i, chunks) * chunk, chunk)
        return pltpu.make_async_copy(
            td.at[pl.ds(first, chunk)], s["d_slot"].at[slot], s["d_sem"].at[slot])

    load_sg = pltpu.make_async_copy(sg, s["w_gate"], s["w_sem"].at[0])
    load_su = pltpu.make_async_copy(su, s["w_gate"], s["w_sem"].at[1])
    load_sd = pltpu.make_async_copy(sd, s["w_down"], s["w_sem"].at[2])
    load_al = pltpu.make_async_copy(al, s["w_align"], s["w_sem"].at[3])

    for c in range(min(TEACHER_SLOTS, chunks)):
        for load in teacher_load(c):
            load.start()
    load_sg.start()
    load_sd.start()
    load_al.start()
    for c in range(min(DOWN_SLOTS, items)):
        down_load(c).start()

    barrier = pltpu.get_barrier_semaphore()
    for other in range(1, tp):
        pl.semaphore_signal(barrier, inc=1, device_id={"tp": lax.rem(me + other, tp)},
                            device_id_type=MESH)
    for other in range(1, role):
        pl.semaphore_signal(barrier, inc=1, device_id={"role": lax.rem(my_role + other, role)},
                            device_id_type=MESH)
    pl.semaphore_wait(barrier, tp + role - 2)

    s["diff"][...] = jnp.zeros_like(s["diff"])

    def rs_copy(way, c, target):
        ref = s["run"].at[way, c]
        return pltpu.make_async_remote_copy(
            src_ref=ref, dst_ref=ref, send_sem=s["run_s"].at[way, c],
            recv_sem=s["run_r"].at[way, c], device_id={"tp": target}, device_id_type=MESH)

    def ag_copy(way, c, target):
        ref = s["hid"].at[c, way]
        return pltpu.make_async_remote_copy(
            src_ref=ref, dst_ref=ref, send_sem=s["hid_s"].at[way, c],
            recv_sem=s["hid_r"].at[way, c], device_id={"tp": target}, device_id_type=MESH)

    def finish_hidden(own, rows):
        tile = width_of(student_units, 1024)
        for j in range(0, student_units, tile):
            gate = s["gate_up"][own, rows, pl.ds(j, tile)]
            up = s["gate_up"][own, rows, pl.ds(student_units + j, tile)]
            s["sh"][own, rows, pl.ds(j, tile)] = (gate * jax.nn.sigmoid(gate) * up).astype(BF16)

    def finish_out(own, rows):
        s["so"][own, rows] = s["narrow"][own, rows].astype(BF16)

    def finish_diff(own, rows):
        s["ga"][own, rows] = (s["diff"][own, rows] * (2.0 * loss_scale / tokens)).astype(BF16)

    def finish_grad_out(own, rows):
        s["gso"][own, rows] = s["narrow"][own, rows].astype(BF16)

    def finish_grad_hidden(own, rows):
        tile = width_of(student_units, 1024)
        for j in range(0, student_units, tile):
            gate = s["gate_up"][own, rows, pl.ds(j, tile)]
            up = s["gate_up"][own, rows, pl.ds(student_units + j, tile)]
            grad = s["diff"][own, rows, pl.ds(j, tile)]
            sigmoid = jax.nn.sigmoid(gate)
            slope = sigmoid * (1.0 + gate * (1.0 - sigmoid))
            s["gg"][own, rows, pl.ds(j, tile)] = (grad * up * slope).astype(BF16)
            s["gu"][own, rows, pl.ds(j, tile)] = (grad * (gate * sigmoid)).astype(BF16)

    wide, narrow = sg.shape[1], sd.shape[1]
    sum_gate = Summed("role", s["gate_up"], 2 * student_units, s["b_gate"], [s["sh"]], finish_hidden)
    sum_out = Summed("tp", s["narrow"], narrow, s["b_out"], [s["so"]], finish_out)
    sum_diff = Summed("role", s["diff"], al.shape[1], s["b_diff"], [s["ga"]], finish_diff)
    sum_grad = Summed("tp", s["narrow"], narrow, s["b_grad"], [s["gso"]], finish_grad_out)
    sum_hidden = Summed("role", s["diff"], wide, s["b_hidden"], [s["gg"], s["gu"]],
                        finish_grad_hidden)

    def product(left, right, out, rows, first_col, columns, transposed, add):
        tile = width_of(columns, 256)

        @pl.loop(0, columns // tile)
        def _(j):
            at = pl.multiple_of(j * tile, tile)
            if transposed:
                block = lax.dot_general(left, right[pl.ds(at, tile)], (((1,), (1,)), ((), ())),
                                        preferred_element_type=F32)
            else:
                block = jnp.dot(left, right[:, pl.ds(at, tile)], preferred_element_type=F32)
            block = block.reshape(2, block.shape[0] // 2, tile)
            cols = pl.ds(pl.multiple_of(first_col + at, tile), tile)
            if add:
                out[:, rows, cols] = out[:, rows, cols] + block
            else:
                out[:, rows, cols] = block

    def student_gate():
        load_sg.wait()
        product(x_s[...], s["w_gate"], s["gate_up"], every, 0, student_units, False, False)
        load_su.start()

    def student_up():
        load_su.wait()
        product(x_s[...], s["w_gate"], s["gate_up"], every, student_units, student_units, False, False)
        sum_gate.phase1()

    def student_down():
        sum_gate.phase4()
        load_sd.wait()
        product(taken(s["sh"], every), s["w_down"], s["narrow"], every, 0, narrow, False, False)
        sum_out.phase1()

    def student_align():
        sum_out.phase4()
        load_al.wait()
        product(taken(s["so"], every), s["w_align"], s["diff"], every, 0, al.shape[1], False, True)

    def grad_out(g):
        sum_diff.phase4(pieces[g])
        product(taken(s["ga"], of_group[g]), s["w_align"], s["narrow"], of_group[g], 0, narrow,
                True, False)
        sum_grad.phase1(pieces[g])

    def grad_hidden(g):
        sum_grad.phase4(pieces[g])
        product(taken(s["gso"], of_group[g]), s["w_down"], s["diff"], of_group[g], 0, wide,
                True, False)
        sum_hidden.phase1(pieces[g])

    first_done = chunks - 1 + 2 * SKEW * last
    plan = {
        1: student_gate, 2: student_up, 4: sum_gate.phase2, 16: sum_gate.phase3,
        18: student_down, 21: sum_out.phase2, 26: sum_out.phase3, 29: student_align,
        first_done: lambda: sum_diff.phase1(pieces[0]),
        first_done + 1: lambda: sum_diff.phase2(pieces[0]),
        first_done + 5: lambda: sum_diff.phase3(pieces[0]),
        first_done + 6: lambda: grad_out(0),
        first_done + 8: lambda: sum_grad.phase2(pieces[0]),
        first_done + 12: lambda: sum_grad.phase3(pieces[0]),
    }
    steps = max(items + 2 * SKEW * last, first_done + 13)

    @pl.loop(0, steps)
    def _(t):
        @pl.when(t < chunks)
        def _():
            for load in teacher_load(t):
                load.wait()
            slot = lax.rem(t, TEACHER_SLOTS)
            for k in range(2):
                block = jnp.dot(x_t[...], s["t_slot"][slot, k], preferred_element_type=F32)
                s["sums"][t, :, :, k * chunk:(k + 1) * chunk] = block.reshape(
                    2, half, chunk)

            @pl.when(t + TEACHER_SLOTS < chunks)
            def _():
                for load in teacher_load(t + TEACHER_SLOTS):
                    load.start()

        for way in range(2):
            hop = last - me if way == 0 else me
            onward = lax.rem(me + (tp - 1 if way == 0 else 1), tp)
            back = lax.rem(me + (1 if way == 0 else tp - 1), tp)
            c = t - SKEW * hop

            @pl.when((c >= 0) & (c < items))
            def _():
                at = lax.rem(c, chunks)
                mine = pl.ds(pl.multiple_of(lax.div(c, chunks) * share, share), share)

                @pl.when(hop == 0)
                def _():
                    s["run"][way, c] = s["sums"][at, way, mine].astype(BF16)
                    rs_copy(way, c, onward).start()

                @pl.when((hop > 0) & (hop < last))
                def _():
                    rs_copy(way, c, onward).wait_recv()
                    s["run"][way, c] = (
                        s["sums"][at, way, mine] + s["run"][way, c].astype(F32)).astype(BF16)
                    rs_copy(way, c, onward).start()

                @pl.when(hop == last)
                def _():
                    rs_copy(way, c, back).wait_recv()
                    gate = s["sums"][at, way, mine, :chunk] + s["run"][way, c, :, :chunk].astype(F32)
                    up = s["sums"][at, way, mine, chunk:] + s["run"][way, c, :, chunk:].astype(F32)
                    s["hid"][c, way] = (gate * jax.nn.sigmoid(gate) * up).astype(BF16)
                    ag_copy(way, c, back).start()

            g = t - SKEW * last - SKEW * (last - hop)

            @pl.when((g >= 0) & (g < items) & (hop < last))
            def _():
                ag_copy(way, g, onward).wait_recv()

                @pl.when(hop > 0)
                def _():
                    ag_copy(way, g, back).start()

        f = t - 2 * SKEW * last

        @pl.when((f >= 0) & (f < items))
        def _():
            down_load(f).wait()
            left = s["hid"][f].reshape(2 * share, chunk)
            mine = pl.ds(pl.multiple_of(lax.div(f, chunks) * share, share), share)
            slot = lax.rem(f, DOWN_SLOTS)
            wide_tile = width_of(td.shape[1], 512)

            @pl.loop(0, td.shape[1] // wide_tile)
            def _(j):
                cols = pl.ds(pl.multiple_of(j * wide_tile, wide_tile), wide_tile)
                block = jnp.dot(left, s["d_slot"][slot, :, cols], preferred_element_type=F32)
                s["diff"][:, mine, cols] = s["diff"][:, mine, cols] - block.reshape(2, share, wide_tile)

            @pl.when(f + DOWN_SLOTS < items)
            def _():
                down_load(f + DOWN_SLOTS).start()

        for at, work in plan.items():
            pl.when(t == at)(work)

    sum_diff.phase1(pieces[1])
    sum_diff.phase2(pieces[1])
    grad_hidden(0)
    sum_hidden.phase2(pieces[0])
    sum_diff.phase3(pieces[1])
    grad_out(1)
    sum_grad.phase2(pieces[1])
    sum_hidden.phase3(pieces[0])
    sum_grad.phase3(pieces[1])
    grad_hidden(1)
    sum_hidden.phase2(pieces[1])

    stores = [
        pltpu.make_async_copy(s[name], out, s["o_sem"].at[i])
        for i, (name, out) in enumerate(
            [("so", o_so), ("ga", o_ga), ("sh", o_sh), ("gso", o_gso), ("gg", o_gg), ("gu", o_gu)])
    ]
    for store in stores[:4]:
        store.start()
    sum_hidden.phase3(pieces[1])
    sum_hidden.phase4()
    for store in stores[4:]:
        store.start()
    sum_gate.drain()
    sum_out.drain()
    sum_diff.drain()
    sum_grad.drain()
    sum_hidden.drain()

    @pl.loop(0, items)
    def _(c):
        for way in range(2):
            hop = last - me if way == 0 else me
            onward = lax.rem(me + (tp - 1 if way == 0 else 1), tp)
            back = lax.rem(me + (1 if way == 0 else tp - 1), tp)

            @pl.when(hop < last)
            def _():
                rs_copy(way, c, onward).wait_send()

            @pl.when(hop > 0)
            def _():
                ag_copy(way, c, back).wait_send()

    for store in stores:
        store.wait()


def exchanged(x_teacher, x_student, t_gate, t_up, t_down, s_gate, s_up, s_down, align):
    tp, role = lax.axis_size("tp"), lax.axis_size("role")
    tokens, depth = x_teacher.shape
    half = tokens // 2
    units = t_gate.shape[1]
    chunk = width_of(units, 256)
    chunks = units // chunk
    items = GROUPS * chunks
    share = half // GROUPS
    wide, narrow, features = s_gate.shape[1], s_down.shape[1], align.shape[1]
    DMA = pltpu.SemaphoreType.DMA
    scratch = dict(
        sums=pltpu.VMEM((chunks, 2, half, 2 * chunk), F32),
        run=pltpu.VMEM((2, items, share, 2 * chunk), BF16),
        run_s=DMA((2, items)), run_r=DMA((2, items)),
        hid=pltpu.VMEM((items, 2, share, chunk), BF16),
        hid_s=DMA((2, items)), hid_r=DMA((2, items)),
        t_slot=pltpu.VMEM((TEACHER_SLOTS, 2, depth, chunk), BF16),
        t_sem=DMA((TEACHER_SLOTS, 2)),
        d_slot=pltpu.VMEM((DOWN_SLOTS, chunk, features), BF16),
        d_sem=DMA((DOWN_SLOTS,)),
        w_gate=pltpu.VMEM(s_gate.shape, BF16),
        w_down=pltpu.VMEM(s_down.shape, BF16),
        w_align=pltpu.VMEM(align.shape, BF16),
        w_sem=DMA((4,)),
        gate_up=pltpu.VMEM((2, half, 2 * wide), F32),
        narrow=pltpu.VMEM((2, half, narrow), F32),
        diff=pltpu.VMEM((2, half, max(features, wide)), F32),
        so=pltpu.VMEM((2, half, narrow), BF16),
        ga=pltpu.VMEM((2, half, features), BF16),
        sh=pltpu.VMEM((2, half, wide), BF16),
        gso=pltpu.VMEM((2, half, narrow), BF16),
        gg=pltpu.VMEM((2, half, wide), BF16),
        gu=pltpu.VMEM((2, half, wide), BF16),
        o_sem=DMA((6,)),
        b_gate=sum_scratch(role, half, 2 * wide, BF16, 1),
        b_out=sum_scratch(tp, half, narrow, BF16, 1),
        b_diff=sum_scratch(role, half, features, BF16, 1),
        b_grad=sum_scratch(tp, half, narrow, BF16, 1),
        b_hidden=sum_scratch(role, half, wide, BF16, 2),
    )
    leaves, names = jax.tree.flatten(scratch, is_leaf=lambda leaf: not isinstance(leaf, dict))
    shapes = [narrow, features, wide, narrow, wide, wide]
    outs = pl.pallas_call(
        functools.partial(exchange_kernel, names, chunk),
        out_shape=[jax.ShapeDtypeStruct((2, half, n), BF16) for n in shapes],
        in_specs=[pl.BlockSpec(memory_space=pltpu.VMEM)] * 2 + [pl.BlockSpec(memory_space=pl.ANY)] * 7,
        out_specs=[pl.BlockSpec(memory_space=pl.ANY)] * 6,
        scratch_shapes=leaves,
        compiler_params=pltpu.CompilerParams(
            collective_id=0, has_side_effects=True, vmem_limit_bytes=60 * 2**20),
        cost_estimate=pl.CostEstimate(flops=20 * 10**9, bytes_accessed=70 * 10**6, transcendentals=10**6),
    )(x_teacher, x_student, t_gate, t_up, t_down, s_gate, s_up, s_down, align)
    return [out.reshape(tokens, out.shape[2]) for out in outs]


def outer_kernel(*refs):
    count = len(refs) // 3
    for i in range(count):
        refs[2 * count + i][...] = lax.dot_general(
            refs[i][...], refs[count + i][...], (((0,), (0,)), ((), ())),
            preferred_element_type=F32).astype(BF16)


def outer_products(lefts, rights):
    tokens = lefts[0].shape[0]
    steps = min(8, min(left.shape[1] for left in lefts) // 128)
    in_specs = [pl.BlockSpec((tokens, left.shape[1] // steps), lambda i: (0, i)) for left in lefts]
    in_specs += [pl.BlockSpec(right.shape, lambda i: (0, 0)) for right in rights]
    return pl.pallas_call(
        outer_kernel,
        grid=(steps,),
        out_shape=[jax.ShapeDtypeStruct((left.shape[1], right.shape[1]), BF16)
                   for left, right in zip(lefts, rights)],
        in_specs=in_specs,
        out_specs=[pl.BlockSpec((left.shape[1] // steps, right.shape[1]), lambda i: (i, 0))
                   for left, right in zip(lefts, rights)],
        compiler_params=pltpu.CompilerParams(vmem_limit_bytes=60 * 2**20),
    )(*lefts, *rights)


def on_device(x_teacher, x_student, *weights):
    student_out, grad_aligned, student_hidden, grad_student_out, grad_gate_pre, grad_up_pre = exchanged(
        x_teacher, x_student, *weights)
    return tuple(outer_products(
        [x_student, x_student, student_hidden, student_out],
        [grad_gate_pre, grad_up_pre, grad_student_out, grad_aligned]))


def solution(mesh):
    placed = (
        P("groups", "tp"),
        P("groups", "role"),
        P("tp", "role"),
        P("tp", "role"),
        P("role", "tp"),
        P("role", "tp"),
        P("role", "tp"),
        P("tp", "role"),
        P("role", "tp"),
    )
    return jax.shard_map(
        on_device,
        mesh=mesh,
        in_specs=placed,
        out_specs=(
            P(("groups", "role"), "tp"),
            P(("groups", "role"), "tp"),
            P(("groups", "tp"), "role"),
            P(("groups", "role"), "tp"),
        ),
        check_vma=False,
    )
```

```python
import functools

import jax
import jax.numpy as jnp
from jax import lax
from jax.experimental import pallas as pl
from jax.experimental.pallas import tpu as pltpu
from jax.sharding import PartitionSpec as P

loss_scale = 16.0
MESH = pl.DeviceIdType.MESH
BF16 = jnp.bfloat16
F32 = jnp.float32
SKEW = 3
GROUPS = 2
TEACHER_SLOTS = 3
DOWN_SLOTS = 3
PIECES = 4


def width_of(columns, wanted):
    width = wanted
    while columns % width:
        width //= 2
    return width


def sum_scratch(devices, half, columns, first_type, finals):
    peers = devices // 2 - 1
    return dict(
        sent1=pltpu.VMEM((half, columns), first_type),
        got1=pltpu.VMEM((half, columns), first_type),
        sent2=pltpu.VMEM((half, columns), BF16),
        got2=pltpu.VMEM((peers, half, columns), BF16),
        s1=pltpu.SemaphoreType.DMA((PIECES,)),
        r1=pltpu.SemaphoreType.DMA((PIECES,)),
        s2=pltpu.SemaphoreType.DMA((peers, PIECES)),
        r2=pltpu.SemaphoreType.DMA((peers, PIECES)),
        s3=pltpu.SemaphoreType.DMA((finals, PIECES)),
        r3=pltpu.SemaphoreType.DMA((finals, PIECES)),
    )


class Summed:
    def __init__(self, axis, part, columns, bufs, finals, finish):
        self.axis = axis
        self.count = lax.axis_size(axis)
        self.me = lax.axis_index(axis)
        self.own = lax.rem(self.me, 2)
        self.pair = self.me + 1 - 2 * self.own
        self.part, self.columns, self.b = part, columns, bufs
        self.finals, self.finish = finals, finish
        self.half = part.shape[1]
        self.step = self.half // PIECES
        self.tile = width_of(columns, 1024)

    def rows(self, k):
        return pl.ds(k * self.step, self.step)

    def tiles(self):
        return [pl.ds(j, self.tile) for j in range(0, self.columns, self.tile)]

    def copy1(self, k):
        rows = self.rows(k)
        return pltpu.make_async_remote_copy(
            src_ref=self.b["sent1"].at[rows], dst_ref=self.b["got1"].at[rows],
            send_sem=self.b["s1"].at[k], recv_sem=self.b["r1"].at[k],
            device_id={self.axis: self.pair}, device_id_type=MESH)

    def copy2(self, j, k):
        rows = self.rows(k)
        return pltpu.make_async_remote_copy(
            src_ref=self.b["sent2"].at[rows], dst_ref=self.b["got2"].at[j, rows],
            send_sem=self.b["s2"].at[j, k], recv_sem=self.b["r2"].at[j, k],
            device_id={self.axis: lax.rem(self.me + 2 * (j + 1), self.count)},
            device_id_type=MESH)

    def copy3(self, i, k, owner):
        rows = self.rows(k)
        ref = self.finals[i].at[owner, rows]
        return pltpu.make_async_remote_copy(
            src_ref=ref, dst_ref=ref,
            send_sem=self.b["s3"].at[i, k], recv_sem=self.b["r3"].at[i, k],
            device_id={self.axis: self.pair}, device_id_type=MESH)

    def phase1(self, pieces=range(PIECES)):
        for k in pieces:
            rows = self.rows(k)
            for cols in self.tiles():
                self.b["sent1"][rows, cols] = self.part[1 - self.own, rows, cols].astype(
                    self.b["sent1"].dtype)
            self.copy1(k).start()

    def phase2(self, pieces=range(PIECES)):
        for k in pieces:
            rows = self.rows(k)
            self.copy1(k).wait_recv()
            for cols in self.tiles():
                total = self.part[self.own, rows, cols] + self.b["got1"][rows, cols].astype(F32)
                self.part[self.own, rows, cols] = total
                self.b["sent2"][rows, cols] = total.astype(BF16)
            for j in range(self.count // 2 - 1):
                self.copy2(j, k).start()

    def phase3(self, pieces=range(PIECES)):
        for k in pieces:
            rows = self.rows(k)
            for j in range(self.count // 2 - 1):
                self.copy2(j, k).wait_recv()
            for cols in self.tiles():
                total = self.part[self.own, rows, cols]
                for j in range(self.count // 2 - 1):
                    total = total + self.b["got2"][j, rows, cols].astype(F32)
                self.part[self.own, rows, cols] = total
            self.finish(self.own, rows)
            for i in range(len(self.finals)):
                self.copy3(i, k, self.own).start()

    def phase4(self, pieces=range(PIECES)):
        for k in pieces:
            for i in range(len(self.finals)):
                self.copy3(i, k, 1 - self.own).wait_recv()

    def drain(self):
        for k in range(PIECES):
            self.copy1(k).wait_send()
            for j in range(self.count // 2 - 1):
                self.copy2(j, k).wait_send()
            for i in range(len(self.finals)):
                self.copy3(i, k, self.own).wait_send()


def taken(ref, rows):
    block = ref[:, rows]
    return block.reshape(block.shape[0] * block.shape[1], block.shape[2])


def exchange_kernel(names, chunk, x_t, x_s, tg, tu, td, sg, su, sd, al,
                    o_so, o_ga, o_sh, o_gso, o_gg, o_gu, *scratch):
    s = jax.tree.unflatten(names, scratch)
    tp, role = lax.axis_size("tp"), lax.axis_size("role")
    me, my_role = lax.axis_index("tp"), lax.axis_index("role")
    tokens = x_t.shape[0]
    half = tokens // 2
    units = tg.shape[1]
    chunks = units // chunk
    student_units = sg.shape[1]
    last = tp - 1
    share = half // GROUPS
    items = GROUPS * chunks
    every = pl.ds(0, half)
    of_group = [pl.ds(g * share, share) for g in range(GROUPS)]
    per_group = PIECES // GROUPS
    pieces = [range(g * per_group, (g + 1) * per_group) for g in range(GROUPS)]

    def teacher_load(c):
        cols = pl.ds(pl.multiple_of(c * chunk, chunk), chunk)
        slot = lax.rem(c, TEACHER_SLOTS)
        return (
            pltpu.make_async_copy(tg.at[:, cols], s["t_slot"].at[slot, 0], s["t_sem"].at[slot, 0]),
            pltpu.make_async_copy(tu.at[:, cols], s["t_slot"].at[slot, 1], s["t_sem"].at[slot, 1]),
        )

    def down_load(i):
        slot = lax.rem(i, DOWN_SLOTS)
        first = pl.multiple_of(lax.rem(i, chunks) * chunk, chunk)
        return pltpu.make_async_copy(
            td.at[pl.ds(first, chunk)], s["d_slot"].at[slot], s["d_sem"].at[slot])

    load_sg = pltpu.make_async_copy(sg, s["w_gate"], s["w_sem"].at[0])
    load_su = pltpu.make_async_copy(su, s["w_gate"], s["w_sem"].at[1])
    load_sd = pltpu.make_async_copy(sd, s["w_down"], s["w_sem"].at[2])
    load_al = pltpu.make_async_copy(al, s["w_align"], s["w_sem"].at[3])

    for c in range(min(TEACHER_SLOTS, chunks)):
        for load in teacher_load(c):
            load.start()
    load_sg.start()
    load_sd.start()
    load_al.start()
    for c in range(min(DOWN_SLOTS, items)):
        down_load(c).start()

    barrier = pltpu.get_barrier_semaphore()
    for other in range(1, tp):
        pl.semaphore_signal(barrier, inc=1, device_id={"tp": lax.rem(me + other, tp)},
                            device_id_type=MESH)
    for other in range(1, role):
        pl.semaphore_signal(barrier, inc=1, device_id={"role": lax.rem(my_role + other, role)},
                            device_id_type=MESH)
    pl.semaphore_wait(barrier, tp + role - 2)

    s["diff"][...] = jnp.zeros_like(s["diff"])

    def rs_copy(way, c, target):
        ref = s["run"].at[way, c]
        return pltpu.make_async_remote_copy(
            src_ref=ref, dst_ref=ref, send_sem=s["run_s"].at[way, c],
            recv_sem=s["run_r"].at[way, c], device_id={"tp": target}, device_id_type=MESH)

    def ag_copy(way, c, target):
        ref = s["hid"].at[c, way]
        return pltpu.make_async_remote_copy(
            src_ref=ref, dst_ref=ref, send_sem=s["hid_s"].at[way, c],
            recv_sem=s["hid_r"].at[way, c], device_id={"tp": target}, device_id_type=MESH)

    def finish_hidden(own, rows):
        tile = width_of(student_units, 1024)
        for j in range(0, student_units, tile):
            gate = s["gate_up"][own, rows, pl.ds(j, tile)]
            up = s["gate_up"][own, rows, pl.ds(student_units + j, tile)]
            s["sh"][own, rows, pl.ds(j, tile)] = (gate * jax.nn.sigmoid(gate) * up).astype(BF16)

    def finish_out(own, rows):
        s["so"][own, rows] = s["narrow"][own, rows].astype(BF16)

    def finish_diff(own, rows):
        s["ga"][own, rows] = (s["diff"][own, rows] * (2.0 * loss_scale / tokens)).astype(BF16)

    def finish_grad_out(own, rows):
        s["gso"][own, rows] = s["narrow"][own, rows].astype(BF16)

    def finish_grad_hidden(own, rows):
        tile = width_of(student_units, 1024)
        for j in range(0, student_units, tile):
            gate = s["gate_up"][own, rows, pl.ds(j, tile)]
            up = s["gate_up"][own, rows, pl.ds(student_units + j, tile)]
            grad = s["diff"][own, rows, pl.ds(j, tile)]
            sigmoid = jax.nn.sigmoid(gate)
            slope = sigmoid * (1.0 + gate * (1.0 - sigmoid))
            s["gg"][own, rows, pl.ds(j, tile)] = (grad * up * slope).astype(BF16)
            s["gu"][own, rows, pl.ds(j, tile)] = (grad * (gate * sigmoid)).astype(BF16)

    wide, narrow = sg.shape[1], sd.shape[1]
    sum_gate = Summed("role", s["gate_up"], 2 * student_units, s["b_gate"], [s["sh"]], finish_hidden)
    sum_out = Summed("tp", s["narrow"], narrow, s["b_out"], [s["so"]], finish_out)
    sum_diff = Summed("role", s["diff"], al.shape[1], s["b_diff"], [s["ga"]], finish_diff)
    sum_grad = Summed("tp", s["narrow"], narrow, s["b_grad"], [s["gso"]], finish_grad_out)
    sum_hidden = Summed("role", s["diff"], wide, s["b_hidden"], [s["gg"], s["gu"]],
                        finish_grad_hidden)

    def product(left, right, out, rows, first_col, columns, transposed, add):
        tile = width_of(columns, 256)

        @pl.loop(0, columns // tile)
        def _(j):
            at = pl.multiple_of(j * tile, tile)
            if transposed:
                block = lax.dot_general(left, right[pl.ds(at, tile)], (((1,), (1,)), ((), ())),
                                        preferred_element_type=F32)
            else:
                block = jnp.dot(left, right[:, pl.ds(at, tile)], preferred_element_type=F32)
            block = block.reshape(2, block.shape[0] // 2, tile)
            cols = pl.ds(pl.multiple_of(first_col + at, tile), tile)
            if add:
                out[:, rows, cols] = out[:, rows, cols] + block
            else:
                out[:, rows, cols] = block

    def student_gate():
        load_sg.wait()
        product(x_s[...], s["w_gate"], s["gate_up"], every, 0, student_units, False, False)
        load_su.start()

    def student_up():
        load_su.wait()
        product(x_s[...], s["w_gate"], s["gate_up"], every, student_units, student_units, False, False)
        sum_gate.phase1()

    def student_down(g):
        sum_gate.phase4(pieces[g])
        if g == 0:
            load_sd.wait()
        product(taken(s["sh"], of_group[g]), s["w_down"], s["narrow"], of_group[g], 0, narrow,
                False, False)
        sum_out.phase1(pieces[g])

    def student_align(g):
        sum_out.phase4(pieces[g])
        if g == 0:
            load_al.wait()
        product(taken(s["so"], of_group[g]), s["w_align"], s["diff"], of_group[g], 0, al.shape[1],
                False, True)

    def grad_out(g):
        sum_diff.phase4(pieces[g])
        product(taken(s["ga"], of_group[g]), s["w_align"], s["narrow"], of_group[g], 0, narrow,
                True, False)
        sum_grad.phase1(pieces[g])

    def grad_hidden(g):
        sum_grad.phase4(pieces[g])
        product(taken(s["gso"], of_group[g]), s["w_down"], s["diff"], of_group[g], 0, wide,
                True, False)
        sum_hidden.phase1(pieces[g])

    first_done = max(chunks - 1 + 2 * SKEW * last, 28)
    plan = [
        (1, student_gate),
        (2, student_up),
        (4, sum_gate.phase2),
        (11, lambda: sum_gate.phase3(pieces[0])),
        (12, lambda: student_down(0)),
        (16, lambda: sum_out.phase2(pieces[0])),
        (18, lambda: sum_gate.phase3(pieces[1])),
        (19, lambda: student_down(1)),
        (22, lambda: sum_out.phase3(pieces[0])),
        (24, lambda: sum_out.phase2(pieces[1])),
        (26, lambda: student_align(0)),
        (30, lambda: sum_out.phase3(pieces[1])),
        (first_done, lambda: sum_diff.phase1(pieces[0])),
        (first_done + 1, lambda: sum_diff.phase2(pieces[0])),
        (34, lambda: student_align(1)),
        (first_done + 6, lambda: sum_diff.phase3(pieces[0])),
        (first_done + 7, lambda: grad_out(0)),
        (first_done + 11, lambda: sum_grad.phase2(pieces[0])),
    ]
    steps = max(items + 2 * SKEW * last, first_done + 12)

    @pl.loop(0, steps)
    def _(t):
        @pl.when(t < chunks)
        def _():
            for load in teacher_load(t):
                load.wait()
            slot = lax.rem(t, TEACHER_SLOTS)
            for k in range(2):
                block = jnp.dot(x_t[...], s["t_slot"][slot, k], preferred_element_type=F32)
                s["sums"][t, :, :, k * chunk:(k + 1) * chunk] = block.reshape(
                    2, half, chunk)

            @pl.when(t + TEACHER_SLOTS < chunks)
            def _():
                for load in teacher_load(t + TEACHER_SLOTS):
                    load.start()

        for way in range(2):
            hop = last - me if way == 0 else me
            onward = lax.rem(me + (tp - 1 if way == 0 else 1), tp)
            back = lax.rem(me + (1 if way == 0 else tp - 1), tp)
            c = t - SKEW * hop

            @pl.when((c >= 0) & (c < items))
            def _():
                at = lax.rem(c, chunks)
                mine = pl.ds(pl.multiple_of(lax.div(c, chunks) * share, share), share)

                @pl.when(hop == 0)
                def _():
                    s["run"][way, c] = s["sums"][at, way, mine].astype(BF16)
                    rs_copy(way, c, onward).start()

                @pl.when((hop > 0) & (hop < last))
                def _():
                    rs_copy(way, c, onward).wait_recv()
                    s["run"][way, c] = (
                        s["sums"][at, way, mine] + s["run"][way, c].astype(F32)).astype(BF16)
                    rs_copy(way, c, onward).start()

                @pl.when(hop == last)
                def _():
                    rs_copy(way, c, back).wait_recv()
                    gate = s["sums"][at, way, mine, :chunk] + s["run"][way, c, :, :chunk].astype(F32)
                    up = s["sums"][at, way, mine, chunk:] + s["run"][way, c, :, chunk:].astype(F32)
                    s["hid"][c, way] = (gate * jax.nn.sigmoid(gate) * up).astype(BF16)
                    ag_copy(way, c, back).start()

            g = t - SKEW * last - SKEW * (last - hop)

            @pl.when((g >= 0) & (g < items) & (hop < last))
            def _():
                ag_copy(way, g, onward).wait_recv()

                @pl.when(hop > 0)
                def _():
                    ag_copy(way, g, back).start()

        f = t - 2 * SKEW * last

        @pl.when((f >= 0) & (f < items))
        def _():
            down_load(f).wait()
            left = s["hid"][f].reshape(2 * share, chunk)
            mine = pl.ds(pl.multiple_of(lax.div(f, chunks) * share, share), share)
            slot = lax.rem(f, DOWN_SLOTS)
            wide_tile = width_of(td.shape[1], 512)

            @pl.loop(0, td.shape[1] // wide_tile)
            def _(j):
                cols = pl.ds(pl.multiple_of(j * wide_tile, wide_tile), wide_tile)
                block = jnp.dot(left, s["d_slot"][slot, :, cols], preferred_element_type=F32)
                s["diff"][:, mine, cols] = s["diff"][:, mine, cols] - block.reshape(2, share, wide_tile)

            @pl.when(f + DOWN_SLOTS < items)
            def _():
                down_load(f + DOWN_SLOTS).start()

        for at, work in plan:
            pl.when(t == at)(work)

    sum_diff.phase1(pieces[1])
    sum_grad.phase3(pieces[0])
    sum_diff.phase2(pieces[1])
    grad_hidden(0)
    sum_hidden.phase2(pieces[0])
    sum_diff.phase3(pieces[1])
    grad_out(1)
    sum_hidden.phase3(pieces[0])
    sum_grad.phase2(pieces[1])
    sum_grad.phase3(pieces[1])
    grad_hidden(1)
    sum_hidden.phase2(pieces[1])

    stores = [
        pltpu.make_async_copy(s[name], out, s["o_sem"].at[i])
        for i, (name, out) in enumerate(
            [("so", o_so), ("ga", o_ga), ("sh", o_sh), ("gso", o_gso), ("gg", o_gg), ("gu", o_gu)])
    ]
    for store in stores[:4]:
        store.start()
    sum_hidden.phase3(pieces[1])
    sum_hidden.phase4()
    for store in stores[4:]:
        store.start()
    sum_gate.drain()
    sum_out.drain()
    sum_diff.drain()
    sum_grad.drain()
    sum_hidden.drain()

    @pl.loop(0, items)
    def _(c):
        for way in range(2):
            hop = last - me if way == 0 else me
            onward = lax.rem(me + (tp - 1 if way == 0 else 1), tp)
            back = lax.rem(me + (1 if way == 0 else tp - 1), tp)

            @pl.when(hop < last)
            def _():
                rs_copy(way, c, onward).wait_send()

            @pl.when(hop > 0)
            def _():
                ag_copy(way, c, back).wait_send()

    for store in stores:
        store.wait()


def exchanged(x_teacher, x_student, t_gate, t_up, t_down, s_gate, s_up, s_down, align):
    tp, role = lax.axis_size("tp"), lax.axis_size("role")
    tokens, depth = x_teacher.shape
    half = tokens // 2
    units = t_gate.shape[1]
    chunk = width_of(units, 256)
    chunks = units // chunk
    items = GROUPS * chunks
    share = half // GROUPS
    wide, narrow, features = s_gate.shape[1], s_down.shape[1], align.shape[1]
    DMA = pltpu.SemaphoreType.DMA
    scratch = dict(
        sums=pltpu.VMEM((chunks, 2, half, 2 * chunk), F32),
        run=pltpu.VMEM((2, items, share, 2 * chunk), BF16),
        run_s=DMA((2, items)), run_r=DMA((2, items)),
        hid=pltpu.VMEM((items, 2, share, chunk), BF16),
        hid_s=DMA((2, items)), hid_r=DMA((2, items)),
        t_slot=pltpu.VMEM((TEACHER_SLOTS, 2, depth, chunk), BF16),
        t_sem=DMA((TEACHER_SLOTS, 2)),
        d_slot=pltpu.VMEM((DOWN_SLOTS, chunk, features), BF16),
        d_sem=DMA((DOWN_SLOTS,)),
        w_gate=pltpu.VMEM(s_gate.shape, BF16),
        w_down=pltpu.VMEM(s_down.shape, BF16),
        w_align=pltpu.VMEM(align.shape, BF16),
        w_sem=DMA((4,)),
        gate_up=pltpu.VMEM((2, half, 2 * wide), F32),
        narrow=pltpu.VMEM((2, half, narrow), F32),
        diff=pltpu.VMEM((2, half, max(features, wide)), F32),
        so=pltpu.VMEM((2, half, narrow), BF16),
        ga=pltpu.VMEM((2, half, features), BF16),
        sh=pltpu.VMEM((2, half, wide), BF16),
        gso=pltpu.VMEM((2, half, narrow), BF16),
        gg=pltpu.VMEM((2, half, wide), BF16),
        gu=pltpu.VMEM((2, half, wide), BF16),
        o_sem=DMA((6,)),
        b_gate=sum_scratch(role, half, 2 * wide, BF16, 1),
        b_out=sum_scratch(tp, half, narrow, BF16, 1),
        b_diff=sum_scratch(role, half, features, BF16, 1),
        b_grad=sum_scratch(tp, half, narrow, BF16, 1),
        b_hidden=sum_scratch(role, half, wide, BF16, 2),
    )
    leaves, names = jax.tree.flatten(scratch, is_leaf=lambda leaf: not isinstance(leaf, dict))
    shapes = [narrow, features, wide, narrow, wide, wide]
    outs = pl.pallas_call(
        functools.partial(exchange_kernel, names, chunk),
        out_shape=[jax.ShapeDtypeStruct((2, half, n), BF16) for n in shapes],
        in_specs=[pl.BlockSpec(memory_space=pltpu.VMEM)] * 2 + [pl.BlockSpec(memory_space=pl.ANY)] * 7,
        out_specs=[pl.BlockSpec(memory_space=pl.ANY)] * 6,
        scratch_shapes=leaves,
        compiler_params=pltpu.CompilerParams(
            collective_id=0, has_side_effects=True, vmem_limit_bytes=60 * 2**20),
        cost_estimate=pl.CostEstimate(flops=20 * 10**9, bytes_accessed=70 * 10**6, transcendentals=10**6),
    )(x_teacher, x_student, t_gate, t_up, t_down, s_gate, s_up, s_down, align)
    return [out.reshape(tokens, out.shape[2]) for out in outs]


def outer_kernel(*refs):
    count = len(refs) // 3
    for i in range(count):
        refs[2 * count + i][...] = lax.dot_general(
            refs[i][...], refs[count + i][...], (((0,), (0,)), ((), ())),
            preferred_element_type=F32).astype(BF16)


def outer_products(lefts, rights):
    tokens = lefts[0].shape[0]
    steps = min(4, min(left.shape[1] for left in lefts) // 128)
    in_specs = [pl.BlockSpec((tokens, left.shape[1] // steps), lambda i: (0, i)) for left in lefts]
    in_specs += [pl.BlockSpec(right.shape, lambda i: (0, 0)) for right in rights]
    return pl.pallas_call(
        outer_kernel,
        grid=(steps,),
        out_shape=[jax.ShapeDtypeStruct((left.shape[1], right.shape[1]), BF16)
                   for left, right in zip(lefts, rights)],
        in_specs=in_specs,
        out_specs=[pl.BlockSpec((left.shape[1] // steps, right.shape[1]), lambda i: (i, 0))
                   for left, right in zip(lefts, rights)],
        compiler_params=pltpu.CompilerParams(vmem_limit_bytes=60 * 2**20),
    )(*lefts, *rights)


def on_device(x_teacher, x_student, *weights):
    student_out, grad_aligned, student_hidden, grad_student_out, grad_gate_pre, grad_up_pre = exchanged(
        x_teacher, x_student, *weights)
    return tuple(outer_products(
        [x_student, x_student, student_hidden, student_out],
        [grad_gate_pre, grad_up_pre, grad_student_out, grad_aligned]))


def solution(mesh):
    placed = (
        P("groups", "tp"),
        P("groups", "role"),
        P("tp", "role"),
        P("tp", "role"),
        P("role", "tp"),
        P("role", "tp"),
        P("role", "tp"),
        P("tp", "role"),
        P("role", "tp"),
    )
    return jax.shard_map(
        on_device,
        mesh=mesh,
        in_specs=placed,
        out_specs=(
            P(("groups", "role"), "tp"),
            P(("groups", "role"), "tp"),
            P(("groups", "tp"), "role"),
            P(("groups", "role"), "tp"),
        ),
        check_vma=False,
    )
```

```python
import functools

import jax
import jax.numpy as jnp
from jax import lax
from jax.experimental import pallas as pl
from jax.experimental.pallas import tpu as pltpu
from jax.sharding import PartitionSpec as P

loss_scale = 16.0
MESH = pl.DeviceIdType.MESH
BF16 = jnp.bfloat16
F32 = jnp.float32
SKEW = 3
GROUPS = 2
TEACHER_SLOTS = 3
DOWN_SLOTS = 3
PIECES = 4


def width_of(columns, wanted):
    width = wanted
    while columns % width:
        width //= 2
    return width


def sum_scratch(devices, half, columns, first_type, finals):
    peers = devices // 2 - 1
    return dict(
        sent1=pltpu.VMEM((half, columns), first_type),
        got1=pltpu.VMEM((half, columns), first_type),
        sent2=pltpu.VMEM((half, columns), BF16),
        got2=pltpu.VMEM((peers, half, columns), BF16),
        s1=pltpu.SemaphoreType.DMA((PIECES,)),
        r1=pltpu.SemaphoreType.DMA((PIECES,)),
        s2=pltpu.SemaphoreType.DMA((peers, PIECES)),
        r2=pltpu.SemaphoreType.DMA((peers, PIECES)),
        s3=pltpu.SemaphoreType.DMA((finals, PIECES)),
        r3=pltpu.SemaphoreType.DMA((finals, PIECES)),
    )


class Summed:
    def __init__(self, axis, part, columns, bufs, finals, finish):
        self.axis = axis
        self.count = lax.axis_size(axis)
        self.me = lax.axis_index(axis)
        self.own = lax.rem(self.me, 2)
        self.pair = self.me + 1 - 2 * self.own
        self.part, self.columns, self.b = part, columns, bufs
        self.finals, self.finish = finals, finish
        self.half = part.shape[1]
        self.step = self.half // PIECES
        self.tile = width_of(columns, 1024)

    def rows(self, k):
        return pl.ds(k * self.step, self.step)

    def tiles(self):
        return [pl.ds(j, self.tile) for j in range(0, self.columns, self.tile)]

    def copy1(self, k):
        rows = self.rows(k)
        return pltpu.make_async_remote_copy(
            src_ref=self.b["sent1"].at[rows], dst_ref=self.b["got1"].at[rows],
            send_sem=self.b["s1"].at[k], recv_sem=self.b["r1"].at[k],
            device_id={self.axis: self.pair}, device_id_type=MESH)

    def copy2(self, j, k):
        rows = self.rows(k)
        return pltpu.make_async_remote_copy(
            src_ref=self.b["sent2"].at[rows], dst_ref=self.b["got2"].at[j, rows],
            send_sem=self.b["s2"].at[j, k], recv_sem=self.b["r2"].at[j, k],
            device_id={self.axis: lax.rem(self.me + 2 * (j + 1), self.count)},
            device_id_type=MESH)

    def copy3(self, i, k, owner):
        rows = self.rows(k)
        ref = self.finals[i].at[owner, rows]
        return pltpu.make_async_remote_copy(
            src_ref=ref, dst_ref=ref,
            send_sem=self.b["s3"].at[i, k], recv_sem=self.b["r3"].at[i, k],
            device_id={self.axis: self.pair}, device_id_type=MESH)

    def phase1(self, pieces=range(PIECES)):
        for k in pieces:
            rows = self.rows(k)
            for cols in self.tiles():
                self.b["sent1"][rows, cols] = self.part[1 - self.own, rows, cols].astype(
                    self.b["sent1"].dtype)
            self.copy1(k).start()

    def phase2(self, pieces=range(PIECES)):
        for k in pieces:
            rows = self.rows(k)
            self.copy1(k).wait_recv()
            for cols in self.tiles():
                total = self.part[self.own, rows, cols] + self.b["got1"][rows, cols].astype(F32)
                self.part[self.own, rows, cols] = total
                self.b["sent2"][rows, cols] = total.astype(BF16)
            for j in range(self.count // 2 - 1):
                self.copy2(j, k).start()

    def phase3(self, pieces=range(PIECES)):
        for k in pieces:
            rows = self.rows(k)
            for j in range(self.count // 2 - 1):
                self.copy2(j, k).wait_recv()
            for cols in self.tiles():
                total = self.part[self.own, rows, cols]
                for j in range(self.count // 2 - 1):
                    total = total + self.b["got2"][j, rows, cols].astype(F32)
                self.part[self.own, rows, cols] = total
            self.finish(self.own, rows)
            for i in range(len(self.finals)):
                self.copy3(i, k, self.own).start()

    def phase4(self, pieces=range(PIECES)):
        for k in pieces:
            for i in range(len(self.finals)):
                self.copy3(i, k, 1 - self.own).wait_recv()

    def drain(self):
        for k in range(PIECES):
            self.copy1(k).wait_send()
            for j in range(self.count // 2 - 1):
                self.copy2(j, k).wait_send()
            for i in range(len(self.finals)):
                self.copy3(i, k, self.own).wait_send()


def taken(ref, rows):
    block = ref[:, rows]
    return block.reshape(block.shape[0] * block.shape[1], block.shape[2])


def exchange_kernel(names, chunk, x_t, x_s, tg, tu, td, sg, su, sd, al,
                    o_so, o_ga, o_sh, o_gso, o_gg, o_gu, *scratch):
    s = jax.tree.unflatten(names, scratch)
    tp, role = lax.axis_size("tp"), lax.axis_size("role")
    me, my_role = lax.axis_index("tp"), lax.axis_index("role")
    tokens = x_t.shape[0]
    half = tokens // 2
    units = tg.shape[1]
    chunks = units // chunk
    student_units = sg.shape[1]
    last = tp - 1
    share = half // GROUPS
    items = GROUPS * chunks
    every = pl.ds(0, half)
    of_group = [pl.ds(g * share, share) for g in range(GROUPS)]
    per_group = PIECES // GROUPS
    pieces = [range(g * per_group, (g + 1) * per_group) for g in range(GROUPS)]

    def teacher_load(c):
        cols = pl.ds(pl.multiple_of(c * chunk, chunk), chunk)
        slot = lax.rem(c, TEACHER_SLOTS)
        return (
            pltpu.make_async_copy(tg.at[:, cols], s["t_slot"].at[slot, :, :chunk], s["t_sem"].at[slot, 0]),
            pltpu.make_async_copy(tu.at[:, cols], s["t_slot"].at[slot, :, chunk:], s["t_sem"].at[slot, 1]),
        )

    def down_load(i):
        slot = lax.rem(i, DOWN_SLOTS)
        first = pl.multiple_of(lax.rem(i, chunks) * chunk, chunk)
        return pltpu.make_async_copy(
            td.at[pl.ds(first, chunk)], s["d_slot"].at[slot], s["d_sem"].at[slot])

    load_sg = pltpu.make_async_copy(sg, s["w_gate"], s["w_sem"].at[0])
    load_su = pltpu.make_async_copy(su, s["w_gate"], s["w_sem"].at[1])
    load_sd = pltpu.make_async_copy(sd, s["w_down"], s["w_sem"].at[2])
    load_al = pltpu.make_async_copy(al, s["w_align"], s["w_sem"].at[3])

    for c in range(min(TEACHER_SLOTS, chunks)):
        for load in teacher_load(c):
            load.start()
    load_sg.start()
    load_sd.start()
    load_al.start()
    for c in range(min(DOWN_SLOTS, items)):
        down_load(c).start()

    barrier = pltpu.get_barrier_semaphore()
    for other in range(1, tp):
        pl.semaphore_signal(barrier, inc=1, device_id={"tp": lax.rem(me + other, tp)},
                            device_id_type=MESH)
    for other in range(1, role):
        pl.semaphore_signal(barrier, inc=1, device_id={"role": lax.rem(my_role + other, role)},
                            device_id_type=MESH)
    pl.semaphore_wait(barrier, tp + role - 2)

    s["diff"][...] = jnp.zeros_like(s["diff"])

    def rs_copy(way, c, target):
        ref = s["run"].at[way, c]
        return pltpu.make_async_remote_copy(
            src_ref=ref, dst_ref=ref, send_sem=s["run_s"].at[way, c],
            recv_sem=s["run_r"].at[way, c], device_id={"tp": target}, device_id_type=MESH)

    def ag_copy(way, c, target):
        ref = s["hid"].at[c, way]
        return pltpu.make_async_remote_copy(
            src_ref=ref, dst_ref=ref, send_sem=s["hid_s"].at[way, c],
            recv_sem=s["hid_r"].at[way, c], device_id={"tp": target}, device_id_type=MESH)

    def finish_hidden(own, rows):
        tile = width_of(student_units, 1024)
        for j in range(0, student_units, tile):
            gate = s["gate_up"][own, rows, pl.ds(j, tile)]
            up = s["gate_up"][own, rows, pl.ds(student_units + j, tile)]
            s["sh"][own, rows, pl.ds(j, tile)] = (gate * jax.nn.sigmoid(gate) * up).astype(BF16)

    def finish_out(own, rows):
        s["so"][own, rows] = s["narrow"][own, rows].astype(BF16)

    def finish_diff(own, rows):
        s["ga"][own, rows] = (s["diff"][own, rows] * (2.0 * loss_scale / tokens)).astype(BF16)

    def finish_grad_out(own, rows):
        s["gso"][own, rows] = s["narrow"][own, rows].astype(BF16)

    def finish_grad_hidden(own, rows):
        tile = width_of(student_units, 1024)
        for j in range(0, student_units, tile):
            gate = s["gate_up"][own, rows, pl.ds(j, tile)]
            up = s["gate_up"][own, rows, pl.ds(student_units + j, tile)]
            grad = s["diff"][own, rows, pl.ds(j, tile)]
            sigmoid = jax.nn.sigmoid(gate)
            slope = sigmoid * (1.0 + gate * (1.0 - sigmoid))
            s["gg"][own, rows, pl.ds(j, tile)] = (grad * up * slope).astype(BF16)
            s["gu"][own, rows, pl.ds(j, tile)] = (grad * (gate * sigmoid)).astype(BF16)

    wide, narrow = sg.shape[1], sd.shape[1]
    sum_gate = Summed("role", s["gate_up"], 2 * student_units, s["b_gate"], [s["sh"]], finish_hidden)
    sum_out = Summed("tp", s["narrow"], narrow, s["b_out"], [s["so"]], finish_out)
    sum_diff = Summed("role", s["diff"], al.shape[1], s["b_diff"], [s["ga"]], finish_diff)
    sum_grad = Summed("tp", s["narrow"], narrow, s["b_grad"], [s["gso"]], finish_grad_out)
    sum_hidden = Summed("role", s["diff"], wide, s["b_hidden"], [s["gg"], s["gu"]],
                        finish_grad_hidden)

    def product(left, right, out, rows, first_col, columns, transposed, add):
        tile = width_of(columns, 512 if transposed else 1024)

        @pl.loop(0, columns // tile)
        def _(j):
            at = pl.multiple_of(j * tile, tile)
            if transposed:
                block = lax.dot_general(left, right[pl.ds(at, tile)], (((1,), (1,)), ((), ())),
                                        preferred_element_type=F32)
            else:
                block = jnp.dot(left, right[:, pl.ds(at, tile)], preferred_element_type=F32)
            block = block.reshape(2, block.shape[0] // 2, tile)
            cols = pl.ds(pl.multiple_of(first_col + at, tile), tile)
            if add:
                out[:, rows, cols] = out[:, rows, cols] + block
            else:
                out[:, rows, cols] = block

    def student_gate():
        load_sg.wait()
        product(x_s[...], s["w_gate"], s["gate_up"], every, 0, student_units, False, False)
        load_su.start()

    def student_up():
        load_su.wait()
        product(x_s[...], s["w_gate"], s["gate_up"], every, student_units, student_units, False, False)
        sum_gate.phase1()

    def student_down(g):
        sum_gate.phase4(pieces[g])
        if g == 0:
            load_sd.wait()
        product(taken(s["sh"], of_group[g]), s["w_down"], s["narrow"], of_group[g], 0, narrow,
                False, False)
        sum_out.phase1(pieces[g])

    def student_align(g):
        sum_out.phase4(pieces[g])
        if g == 0:
            load_al.wait()
        product(taken(s["so"], of_group[g]), s["w_align"], s["diff"], of_group[g], 0, al.shape[1],
                False, True)

    def rows_of(some):
        step = half // PIECES
        return pl.ds(some[0] * step, len(some) * step)

    def grad_out(some):
        rows = rows_of(some)
        sum_diff.phase4(some)
        product(taken(s["ga"], rows), s["w_align"], s["narrow"], rows, 0, narrow, True, False)
        sum_grad.phase1(some)

    def grad_hidden(some):
        rows = rows_of(some)
        sum_grad.phase4(some)
        product(taken(s["gso"], rows), s["w_down"], s["diff"], rows, 0, wide, True, False)
        sum_hidden.phase1(some)

    first_done = max(chunks - 1 + 2 * SKEW * last, 28)
    plan = [
        (1, student_gate),
        (2, student_up),
        (4, sum_gate.phase2),
        (11, lambda: sum_gate.phase3(pieces[0])),
        (12, lambda: student_down(0)),
        (16, lambda: sum_out.phase2(pieces[0])),
        (18, lambda: sum_gate.phase3(pieces[1])),
        (19, lambda: student_down(1)),
        (22, lambda: sum_out.phase3(pieces[0])),
        (24, lambda: sum_out.phase2(pieces[1])),
        (26, lambda: student_align(0)),
        (30, lambda: sum_out.phase3(pieces[1])),
        (first_done, lambda: sum_diff.phase1(pieces[0])),
        (first_done + 1, lambda: sum_diff.phase2(pieces[0])),
        (34, lambda: student_align(1)),
        (first_done + 5, lambda: sum_diff.phase3(pieces[0])),
        (first_done + 6, lambda: grad_out(pieces[0])),
        (first_done + 9, lambda: sum_grad.phase2(pieces[0])),
        (first_done + 13, lambda: sum_grad.phase3(pieces[0])),
    ]
    steps = max(items + 2 * SKEW * last, first_done + 14)

    @pl.loop(0, steps)
    def _(t):
        @pl.when(t < chunks)
        def _():
            for load in teacher_load(t):
                load.wait()
            slot = lax.rem(t, TEACHER_SLOTS)
            block = jnp.dot(x_t[...], s["t_slot"][slot], preferred_element_type=F32)
            s["sums"][t] = block.reshape(2, half, 2 * chunk)

            @pl.when(t + TEACHER_SLOTS < chunks)
            def _():
                for load in teacher_load(t + TEACHER_SLOTS):
                    load.start()

        for way in range(2):
            hop = last - me if way == 0 else me
            onward = lax.rem(me + (tp - 1 if way == 0 else 1), tp)
            back = lax.rem(me + (1 if way == 0 else tp - 1), tp)
            c = t - SKEW * hop

            @pl.when((c >= 0) & (c < items))
            def _():
                at = lax.rem(c, chunks)
                mine = pl.ds(pl.multiple_of(lax.div(c, chunks) * share, share), share)

                @pl.when(hop == 0)
                def _():
                    s["run"][way, c] = s["sums"][at, way, mine].astype(BF16)
                    rs_copy(way, c, onward).start()

                @pl.when((hop > 0) & (hop < last))
                def _():
                    rs_copy(way, c, onward).wait_recv()
                    s["run"][way, c] = (
                        s["sums"][at, way, mine] + s["run"][way, c].astype(F32)).astype(BF16)
                    rs_copy(way, c, onward).start()

                @pl.when(hop == last)
                def _():
                    rs_copy(way, c, back).wait_recv()
                    gate = s["sums"][at, way, mine, :chunk] + s["run"][way, c, :, :chunk].astype(F32)
                    up = s["sums"][at, way, mine, chunk:] + s["run"][way, c, :, chunk:].astype(F32)
                    s["hid"][c, way] = (gate * jax.nn.sigmoid(gate) * up).astype(BF16)
                    ag_copy(way, c, back).start()

            g = t - SKEW * last - SKEW * (last - hop)

            @pl.when((g >= 0) & (g < items) & (hop < last))
            def _():
                ag_copy(way, g, onward).wait_recv()

                @pl.when(hop > 0)
                def _():
                    ag_copy(way, g, back).start()

        f = t - 2 * SKEW * last

        @pl.when((f >= 0) & (f < items))
        def _():
            down_load(f).wait()
            left = s["hid"][f].reshape(2 * share, chunk)
            mine = pl.ds(pl.multiple_of(lax.div(f, chunks) * share, share), share)
            slot = lax.rem(f, DOWN_SLOTS)
            wide_tile = width_of(td.shape[1], 2048)

            @pl.loop(0, td.shape[1] // wide_tile)
            def _(j):
                cols = pl.ds(pl.multiple_of(j * wide_tile, wide_tile), wide_tile)
                block = jnp.dot(left, s["d_slot"][slot, :, cols], preferred_element_type=F32)
                s["diff"][:, mine, cols] = s["diff"][:, mine, cols] - block.reshape(2, share, wide_tile)

            @pl.when(f + DOWN_SLOTS < items)
            def _():
                down_load(f + DOWN_SLOTS).start()

        for at, work in plan:
            pl.when(t == at)(work)

    single = [[k] for k in pieces[1]]
    sum_diff.phase1(pieces[1])
    sum_diff.phase2(pieces[1])
    grad_hidden(pieces[0])
    sum_hidden.phase2(pieces[0])
    for k in single:
        sum_diff.phase3(k)
    for k in single:
        grad_out(k)
    sum_hidden.phase3(pieces[0])
    for k in single:
        sum_grad.phase2(k)
    for k in single:
        sum_grad.phase3(k)
    for k in single:
        grad_hidden(k)
    for k in single:
        sum_hidden.phase2(k)

    stores = [
        pltpu.make_async_copy(s[name], out, s["o_sem"].at[i])
        for i, (name, out) in enumerate(
            [("so", o_so), ("ga", o_ga), ("sh", o_sh), ("gso", o_gso), ("gg", o_gg), ("gu", o_gu)])
    ]
    for store in stores[:4]:
        store.start()
    sum_hidden.phase3(pieces[1])
    sum_hidden.phase4()
    for store in stores[4:]:
        store.start()
    sum_gate.drain()
    sum_out.drain()
    sum_diff.drain()
    sum_grad.drain()
    sum_hidden.drain()

    @pl.loop(0, items)
    def _(c):
        for way in range(2):
            hop = last - me if way == 0 else me
            onward = lax.rem(me + (tp - 1 if way == 0 else 1), tp)
            back = lax.rem(me + (1 if way == 0 else tp - 1), tp)

            @pl.when(hop < last)
            def _():
                rs_copy(way, c, onward).wait_send()

            @pl.when(hop > 0)
            def _():
                ag_copy(way, c, back).wait_send()

    for store in stores:
        store.wait()


def exchanged(x_teacher, x_student, t_gate, t_up, t_down, s_gate, s_up, s_down, align):
    tp, role = lax.axis_size("tp"), lax.axis_size("role")
    tokens, depth = x_teacher.shape
    half = tokens // 2
    units = t_gate.shape[1]
    chunk = width_of(units, 256)
    chunks = units // chunk
    items = GROUPS * chunks
    share = half // GROUPS
    wide, narrow, features = s_gate.shape[1], s_down.shape[1], align.shape[1]
    DMA = pltpu.SemaphoreType.DMA
    scratch = dict(
        sums=pltpu.VMEM((chunks, 2, half, 2 * chunk), F32),
        run=pltpu.VMEM((2, items, share, 2 * chunk), BF16),
        run_s=DMA((2, items)), run_r=DMA((2, items)),
        hid=pltpu.VMEM((items, 2, share, chunk), BF16),
        hid_s=DMA((2, items)), hid_r=DMA((2, items)),
        t_slot=pltpu.VMEM((TEACHER_SLOTS, depth, 2 * chunk), BF16),
        t_sem=DMA((TEACHER_SLOTS, 2)),
        d_slot=pltpu.VMEM((DOWN_SLOTS, chunk, features), BF16),
        d_sem=DMA((DOWN_SLOTS,)),
        w_gate=pltpu.VMEM(s_gate.shape, BF16),
        w_down=pltpu.VMEM(s_down.shape, BF16),
        w_align=pltpu.VMEM(align.shape, BF16),
        w_sem=DMA((4,)),
        gate_up=pltpu.VMEM((2, half, 2 * wide), F32),
        narrow=pltpu.VMEM((2, half, narrow), F32),
        diff=pltpu.VMEM((2, half, max(features, wide)), F32),
        so=pltpu.VMEM((2, half, narrow), BF16),
        ga=pltpu.VMEM((2, half, features), BF16),
        sh=pltpu.VMEM((2, half, wide), BF16),
        gso=pltpu.VMEM((2, half, narrow), BF16),
        gg=pltpu.VMEM((2, half, wide), BF16),
        gu=pltpu.VMEM((2, half, wide), BF16),
        o_sem=DMA((6,)),
        b_gate=sum_scratch(role, half, 2 * wide, BF16, 1),
        b_out=sum_scratch(tp, half, narrow, BF16, 1),
        b_diff=sum_scratch(role, half, features, BF16, 1),
        b_grad=sum_scratch(tp, half, narrow, BF16, 1),
        b_hidden=sum_scratch(role, half, wide, BF16, 2),
    )
    leaves, names = jax.tree.flatten(scratch, is_leaf=lambda leaf: not isinstance(leaf, dict))
    shapes = [narrow, features, wide, narrow, wide, wide]
    outs = pl.pallas_call(
        functools.partial(exchange_kernel, names, chunk),
        out_shape=[jax.ShapeDtypeStruct((2, half, n), BF16) for n in shapes],
        in_specs=[pl.BlockSpec(memory_space=pltpu.VMEM)] * 2 + [pl.BlockSpec(memory_space=pl.ANY)] * 7,
        out_specs=[pl.BlockSpec(memory_space=pl.ANY)] * 6,
        scratch_shapes=leaves,
        compiler_params=pltpu.CompilerParams(
            collective_id=0, has_side_effects=True, vmem_limit_bytes=60 * 2**20),
        cost_estimate=pl.CostEstimate(flops=20 * 10**9, bytes_accessed=70 * 10**6, transcendentals=10**6),
    )(x_teacher, x_student, t_gate, t_up, t_down, s_gate, s_up, s_down, align)
    return [out.reshape(tokens, out.shape[2]) for out in outs]


def outer_kernel(*refs):
    count = len(refs) // 3
    for i in range(count):
        refs[2 * count + i][...] = lax.dot_general(
            refs[i][...], refs[count + i][...], (((0,), (0,)), ((), ())),
            preferred_element_type=F32).astype(BF16)


def outer_products(lefts, rights):
    tokens = lefts[0].shape[0]
    steps = min(4, min(left.shape[1] for left in lefts) // 128)
    in_specs = [pl.BlockSpec((tokens, left.shape[1] // steps), lambda i: (0, i)) for left in lefts]
    in_specs += [pl.BlockSpec(right.shape, lambda i: (0, 0)) for right in rights]
    return pl.pallas_call(
        outer_kernel,
        grid=(steps,),
        out_shape=[jax.ShapeDtypeStruct((left.shape[1], right.shape[1]), BF16)
                   for left, right in zip(lefts, rights)],
        in_specs=in_specs,
        out_specs=[pl.BlockSpec((left.shape[1] // steps, right.shape[1]), lambda i: (i, 0))
                   for left, right in zip(lefts, rights)],
        compiler_params=pltpu.CompilerParams(vmem_limit_bytes=60 * 2**20),
    )(*lefts, *rights)


def on_device(x_teacher, x_student, *weights):
    student_out, grad_aligned, student_hidden, grad_student_out, grad_gate_pre, grad_up_pre = exchanged(
        x_teacher, x_student, *weights)
    return tuple(outer_products(
        [x_student, x_student, student_hidden, student_out],
        [grad_gate_pre, grad_up_pre, grad_student_out, grad_aligned]))


def solution(mesh):
    placed = (
        P("groups", "tp"),
        P("groups", "role"),
        P("tp", "role"),
        P("tp", "role"),
        P("role", "tp"),
        P("role", "tp"),
        P("role", "tp"),
        P("tp", "role"),
        P("role", "tp"),
    )
    return jax.shard_map(
        on_device,
        mesh=mesh,
        in_specs=placed,
        out_specs=(
            P(("groups", "role"), "tp"),
            P(("groups", "role"), "tp"),
            P(("groups", "tp"), "role"),
            P(("groups", "role"), "tp"),
        ),
        check_vma=False,
    )
```

```python
import functools

import jax
import jax.numpy as jnp
from jax import lax
from jax.experimental import pallas as pl
from jax.experimental.pallas import tpu as pltpu
from jax.sharding import PartitionSpec as P

loss_scale = 16.0
MESH = pl.DeviceIdType.MESH
BF16 = jnp.bfloat16
F32 = jnp.float32
SKEW = 3
GROUPS = 4
TEACHER_SLOTS = 3
DOWN_SLOTS = 3
PIECES = 4


def width_of(columns, wanted):
    width = wanted
    while columns % width:
        width //= 2
    return width


def sum_scratch(devices, half, columns, first_type, finals):
    peers = devices // 2 - 1
    return dict(
        sent1=pltpu.VMEM((half, columns), first_type),
        got1=pltpu.VMEM((half, columns), first_type),
        sent2=pltpu.VMEM((half, columns), BF16),
        got2=pltpu.VMEM((peers, half, columns), BF16),
        s1=pltpu.SemaphoreType.DMA((PIECES,)),
        r1=pltpu.SemaphoreType.DMA((PIECES,)),
        s2=pltpu.SemaphoreType.DMA((peers, PIECES)),
        r2=pltpu.SemaphoreType.DMA((peers, PIECES)),
        s3=pltpu.SemaphoreType.DMA((finals, PIECES)),
        r3=pltpu.SemaphoreType.DMA((finals, PIECES)),
    )


class Summed:
    def __init__(self, axis, part, columns, bufs, finals, finish):
        self.axis = axis
        self.count = lax.axis_size(axis)
        self.me = lax.axis_index(axis)
        self.own = lax.rem(self.me, 2)
        self.pair = self.me + 1 - 2 * self.own
        self.part, self.columns, self.b = part, columns, bufs
        self.finals, self.finish = finals, finish
        self.half = part.shape[1]
        self.step = self.half // PIECES
        self.tile = width_of(columns, 1024)

    def rows(self, k):
        return pl.ds(k * self.step, self.step)

    def tiles(self):
        return [pl.ds(j, self.tile) for j in range(0, self.columns, self.tile)]

    def copy1(self, k):
        rows = self.rows(k)
        return pltpu.make_async_remote_copy(
            src_ref=self.b["sent1"].at[rows], dst_ref=self.b["got1"].at[rows],
            send_sem=self.b["s1"].at[k], recv_sem=self.b["r1"].at[k],
            device_id={self.axis: self.pair}, device_id_type=MESH)

    def copy2(self, j, k):
        rows = self.rows(k)
        return pltpu.make_async_remote_copy(
            src_ref=self.b["sent2"].at[rows], dst_ref=self.b["got2"].at[j, rows],
            send_sem=self.b["s2"].at[j, k], recv_sem=self.b["r2"].at[j, k],
            device_id={self.axis: lax.rem(self.me + 2 * (j + 1), self.count)},
            device_id_type=MESH)

    def copy3(self, i, k, owner):
        rows = self.rows(k)
        ref = self.finals[i].at[owner, rows]
        return pltpu.make_async_remote_copy(
            src_ref=ref, dst_ref=ref,
            send_sem=self.b["s3"].at[i, k], recv_sem=self.b["r3"].at[i, k],
            device_id={self.axis: self.pair}, device_id_type=MESH)

    def phase1(self, pieces=range(PIECES)):
        for k in pieces:
            rows = self.rows(k)
            for cols in self.tiles():
                self.b["sent1"][rows, cols] = self.part[1 - self.own, rows, cols].astype(
                    self.b["sent1"].dtype)
            self.copy1(k).start()

    def phase2(self, pieces=range(PIECES)):
        for k in pieces:
            rows = self.rows(k)
            self.copy1(k).wait_recv()
            for cols in self.tiles():
                total = self.part[self.own, rows, cols] + self.b["got1"][rows, cols].astype(F32)
                self.part[self.own, rows, cols] = total
                self.b["sent2"][rows, cols] = total.astype(BF16)
            for j in range(self.count // 2 - 1):
                self.copy2(j, k).start()

    def phase3(self, pieces=range(PIECES)):
        for k in pieces:
            rows = self.rows(k)
            for j in range(self.count // 2 - 1):
                self.copy2(j, k).wait_recv()
            for cols in self.tiles():
                total = self.part[self.own, rows, cols]
                for j in range(self.count // 2 - 1):
                    total = total + self.b["got2"][j, rows, cols].astype(F32)
                self.part[self.own, rows, cols] = total
            self.finish(self.own, rows)
            for i in range(len(self.finals)):
                self.copy3(i, k, self.own).start()

    def phase4(self, pieces=range(PIECES)):
        for k in pieces:
            for i in range(len(self.finals)):
                self.copy3(i, k, 1 - self.own).wait_recv()

    def drain(self):
        for k in range(PIECES):
            self.copy1(k).wait_send()
            for j in range(self.count // 2 - 1):
                self.copy2(j, k).wait_send()
            for i in range(len(self.finals)):
                self.copy3(i, k, self.own).wait_send()


def taken(ref, rows):
    block = ref[:, rows]
    return block.reshape(block.shape[0] * block.shape[1], block.shape[2])


def exchange_kernel(names, chunk, x_t, x_s, tg, tu, td, sg, su, sd, al,
                    o_so, o_ga, o_sh, o_gso, o_gg, o_gu, *scratch):
    s = jax.tree.unflatten(names, scratch)
    tp, role = lax.axis_size("tp"), lax.axis_size("role")
    me, my_role = lax.axis_index("tp"), lax.axis_index("role")
    tokens = x_t.shape[0]
    half = tokens // 2
    units = tg.shape[1]
    chunks = units // chunk
    student_units = sg.shape[1]
    last = tp - 1
    share = half // GROUPS
    items = GROUPS * chunks
    every = pl.ds(0, half)
    of_group = [pl.ds(g * (half // 2), half // 2) for g in range(2)]
    pieces = [range(g * PIECES // 2, (g + 1) * PIECES // 2) for g in range(2)]
    per_group = PIECES // GROUPS
    group = [range(g * per_group, (g + 1) * per_group) for g in range(GROUPS)]

    def teacher_load(c):
        cols = pl.ds(pl.multiple_of(c * chunk, chunk), chunk)
        slot = lax.rem(c, TEACHER_SLOTS)
        return (
            pltpu.make_async_copy(tg.at[:, cols], s["t_slot"].at[slot, :, :chunk], s["t_sem"].at[slot, 0]),
            pltpu.make_async_copy(tu.at[:, cols], s["t_slot"].at[slot, :, chunk:], s["t_sem"].at[slot, 1]),
        )

    def down_load(i):
        slot = lax.rem(i, DOWN_SLOTS)
        first = pl.multiple_of(lax.rem(i, chunks) * chunk, chunk)
        return pltpu.make_async_copy(
            td.at[pl.ds(first, chunk)], s["d_slot"].at[slot], s["d_sem"].at[slot])

    load_sg = pltpu.make_async_copy(sg, s["w_gate"], s["w_sem"].at[0])
    load_su = pltpu.make_async_copy(su, s["w_gate"], s["w_sem"].at[1])
    load_sd = pltpu.make_async_copy(sd, s["w_down"], s["w_sem"].at[2])
    load_al = pltpu.make_async_copy(al, s["w_align"], s["w_sem"].at[3])

    for c in range(min(TEACHER_SLOTS, chunks)):
        for load in teacher_load(c):
            load.start()
    load_sg.start()
    load_sd.start()
    load_al.start()
    for c in range(min(DOWN_SLOTS, items)):
        down_load(c).start()

    barrier = pltpu.get_barrier_semaphore()
    for other in range(1, tp):
        pl.semaphore_signal(barrier, inc=1, device_id={"tp": lax.rem(me + other, tp)},
                            device_id_type=MESH)
    for other in range(1, role):
        pl.semaphore_signal(barrier, inc=1, device_id={"role": lax.rem(my_role + other, role)},
                            device_id_type=MESH)
    pl.semaphore_wait(barrier, tp + role - 2)

    s["diff"][...] = jnp.zeros_like(s["diff"])

    def rs_copy(way, c, target):
        ref = s["run"].at[way, c]
        return pltpu.make_async_remote_copy(
            src_ref=ref, dst_ref=ref, send_sem=s["run_s"].at[way, c],
            recv_sem=s["run_r"].at[way, c], device_id={"tp": target}, device_id_type=MESH)

    def ag_copy(way, c, target):
        ref = s["hid"].at[c, way]
        return pltpu.make_async_remote_copy(
            src_ref=ref, dst_ref=ref, send_sem=s["hid_s"].at[way, c],
            recv_sem=s["hid_r"].at[way, c], device_id={"tp": target}, device_id_type=MESH)

    def finish_hidden(own, rows):
        tile = width_of(student_units, 1024)
        for j in range(0, student_units, tile):
            gate = s["gate_up"][own, rows, pl.ds(j, tile)]
            up = s["gate_up"][own, rows, pl.ds(student_units + j, tile)]
            s["sh"][own, rows, pl.ds(j, tile)] = (gate * jax.nn.sigmoid(gate) * up).astype(BF16)

    def finish_out(own, rows):
        s["so"][own, rows] = s["narrow"][own, rows].astype(BF16)

    def finish_diff(own, rows):
        s["ga"][own, rows] = (s["diff"][own, rows] * (2.0 * loss_scale / tokens)).astype(BF16)

    def finish_grad_out(own, rows):
        s["gso"][own, rows] = s["narrow"][own, rows].astype(BF16)

    def finish_grad_hidden(own, rows):
        tile = width_of(student_units, 1024)
        for j in range(0, student_units, tile):
            gate = s["gate_up"][own, rows, pl.ds(j, tile)]
            up = s["gate_up"][own, rows, pl.ds(student_units + j, tile)]
            grad = s["diff"][own, rows, pl.ds(j, tile)]
            sigmoid = jax.nn.sigmoid(gate)
            slope = sigmoid * (1.0 + gate * (1.0 - sigmoid))
            s["gg"][own, rows, pl.ds(j, tile)] = (grad * up * slope).astype(BF16)
            s["gu"][own, rows, pl.ds(j, tile)] = (grad * (gate * sigmoid)).astype(BF16)

    wide, narrow = sg.shape[1], sd.shape[1]
    sum_gate = Summed("role", s["gate_up"], 2 * student_units, s["b_gate"], [s["sh"]], finish_hidden)
    sum_out = Summed("tp", s["narrow"], narrow, s["b_out"], [s["so"]], finish_out)
    sum_diff = Summed("role", s["diff"], al.shape[1], s["b_diff"], [s["ga"]], finish_diff)
    sum_grad = Summed("tp", s["narrow"], narrow, s["b_grad"], [s["gso"]], finish_grad_out)
    sum_hidden = Summed("role", s["diff"], wide, s["b_hidden"], [s["gg"], s["gu"]],
                        finish_grad_hidden)

    def product(left, right, out, rows, first_col, columns, transposed, add):
        tile = width_of(columns, 512 if transposed else 1024)

        @pl.loop(0, columns // tile)
        def _(j):
            at = pl.multiple_of(j * tile, tile)
            if transposed:
                block = lax.dot_general(left, right[pl.ds(at, tile)], (((1,), (1,)), ((), ())),
                                        preferred_element_type=F32)
            else:
                block = jnp.dot(left, right[:, pl.ds(at, tile)], preferred_element_type=F32)
            block = block.reshape(2, block.shape[0] // 2, tile)
            cols = pl.ds(pl.multiple_of(first_col + at, tile), tile)
            if add:
                out[:, rows, cols] = out[:, rows, cols] + block
            else:
                out[:, rows, cols] = block

    def student_gate():
        load_sg.wait()
        product(x_s[...], s["w_gate"], s["gate_up"], every, 0, student_units, False, False)
        load_su.start()

    def student_up():
        load_su.wait()
        product(x_s[...], s["w_gate"], s["gate_up"], every, student_units, student_units, False, False)
        sum_gate.phase1()

    def student_down(g):
        sum_gate.phase4(pieces[g])
        if g == 0:
            load_sd.wait()
        product(taken(s["sh"], of_group[g]), s["w_down"], s["narrow"], of_group[g], 0, narrow,
                False, False)
        sum_out.phase1(pieces[g])

    def student_align(g):
        sum_out.phase4(pieces[g])
        if g == 0:
            load_al.wait()
        product(taken(s["so"], of_group[g]), s["w_align"], s["diff"], of_group[g], 0, al.shape[1],
                False, True)

    def rows_of(some):
        step = half // PIECES
        return pl.ds(some[0] * step, len(some) * step)

    def grad_out(some):
        rows = rows_of(some)
        sum_diff.phase4(some)
        product(taken(s["ga"], rows), s["w_align"], s["narrow"], rows, 0, narrow, True, False)
        sum_grad.phase1(some)

    def grad_hidden(some):
        rows = rows_of(some)
        sum_grad.phase4(some)
        product(taken(s["gso"], rows), s["w_down"], s["diff"], rows, 0, wide, True, False)
        sum_hidden.phase1(some)

    plan = [
        (1, student_gate),
        (2, student_up),
        (4, sum_gate.phase2),
        (13, lambda: sum_gate.phase3(pieces[0])),
        (14, lambda: student_down(0)),
        (19, lambda: sum_out.phase2(pieces[0])),
        (22, lambda: sum_gate.phase3(pieces[1])),
        (23, lambda: student_down(1)),
        (27, lambda: sum_out.phase3(pieces[0])),
        (29, lambda: sum_out.phase2(pieces[1])),
        (32, lambda: student_align(0)),
        (38, lambda: sum_out.phase3(pieces[1])),
        (39, lambda: student_align(1)),
    ]
    for g in range(GROUPS - 1):
        start = max((g + 1) * chunks - 1 + 2 * SKEW * last, 40)
        some = group[g]
        plan += [
            (start, functools.partial(sum_diff.phase1, some)),
            (start + 1, functools.partial(sum_diff.phase2, some)),
            (start + 5, functools.partial(sum_diff.phase3, some)),
            (start + 6, functools.partial(grad_out, some)),
            (start + 9, functools.partial(sum_grad.phase2, some)),
            (start + 13, functools.partial(sum_grad.phase3, some)),
        ]
        if g < GROUPS - 2:
            plan += [
                (start + 14, functools.partial(grad_hidden, some)),
                (start + 15, functools.partial(sum_hidden.phase2, some)),
                (start + 20, functools.partial(sum_hidden.phase3, some)),
            ]
    steps = max([items + 2 * SKEW * last] + [at + 1 for at, _ in plan])

    @pl.loop(0, steps)
    def _(t):
        @pl.when(t < chunks)
        def _():
            for load in teacher_load(t):
                load.wait()
            slot = lax.rem(t, TEACHER_SLOTS)
            block = jnp.dot(x_t[...], s["t_slot"][slot], preferred_element_type=F32)
            s["sums"][t] = block.reshape(2, half, 2 * chunk)

            @pl.when(t + TEACHER_SLOTS < chunks)
            def _():
                for load in teacher_load(t + TEACHER_SLOTS):
                    load.start()

        for way in range(2):
            hop = last - me if way == 0 else me
            onward = lax.rem(me + (tp - 1 if way == 0 else 1), tp)
            back = lax.rem(me + (1 if way == 0 else tp - 1), tp)
            c = t - SKEW * hop

            @pl.when((c >= 0) & (c < items))
            def _():
                at = lax.rem(c, chunks)
                mine = pl.ds(pl.multiple_of(lax.div(c, chunks) * share, share), share)

                @pl.when(hop == 0)
                def _():
                    s["run"][way, c] = s["sums"][at, way, mine].astype(BF16)
                    rs_copy(way, c, onward).start()

                @pl.when((hop > 0) & (hop < last))
                def _():
                    rs_copy(way, c, onward).wait_recv()
                    s["run"][way, c] = (
                        s["sums"][at, way, mine] + s["run"][way, c].astype(F32)).astype(BF16)
                    rs_copy(way, c, onward).start()

                @pl.when(hop == last)
                def _():
                    rs_copy(way, c, back).wait_recv()
                    gate = s["sums"][at, way, mine, :chunk] + s["run"][way, c, :, :chunk].astype(F32)
                    up = s["sums"][at, way, mine, chunk:] + s["run"][way, c, :, chunk:].astype(F32)
                    s["hid"][c, way] = (gate * jax.nn.sigmoid(gate) * up).astype(BF16)
                    ag_copy(way, c, back).start()

            g = t - SKEW * last - SKEW * (last - hop)

            @pl.when((g >= 0) & (g < items) & (hop < last))
            def _():
                ag_copy(way, g, onward).wait_recv()

                @pl.when(hop > 0)
                def _():
                    ag_copy(way, g, back).start()

        f = t - 2 * SKEW * last

        @pl.when((f >= 0) & (f < items))
        def _():
            down_load(f).wait()
            left = s["hid"][f].reshape(2 * share, chunk)
            mine = pl.ds(pl.multiple_of(lax.div(f, chunks) * share, share), share)
            slot = lax.rem(f, DOWN_SLOTS)
            wide_tile = width_of(td.shape[1], 2048)

            @pl.loop(0, td.shape[1] // wide_tile)
            def _(j):
                cols = pl.ds(pl.multiple_of(j * wide_tile, wide_tile), wide_tile)
                block = jnp.dot(left, s["d_slot"][slot, :, cols], preferred_element_type=F32)
                s["diff"][:, mine, cols] = s["diff"][:, mine, cols] - block.reshape(2, share, wide_tile)

            @pl.when(f + DOWN_SLOTS < items)
            def _():
                down_load(f + DOWN_SLOTS).start()

        for at, work in plan:
            pl.when(t == at)(work)

    late, final = group[-2], group[-1]
    sum_diff.phase1(final)
    sum_diff.phase2(final)
    grad_hidden(late)
    sum_hidden.phase2(late)
    sum_diff.phase3(final)
    grad_out(final)
    sum_hidden.phase3(late)
    sum_grad.phase2(final)
    sum_grad.phase3(final)
    grad_hidden(final)
    sum_hidden.phase2(final)

    stores = [
        pltpu.make_async_copy(s[name], out, s["o_sem"].at[i])
        for i, (name, out) in enumerate(
            [("so", o_so), ("ga", o_ga), ("sh", o_sh), ("gso", o_gso), ("gg", o_gg), ("gu", o_gu)])
    ]
    for store in stores[:4]:
        store.start()
    sum_hidden.phase3(final)
    sum_hidden.phase4()
    for store in stores[4:]:
        store.start()
    sum_gate.drain()
    sum_out.drain()
    sum_diff.drain()
    sum_grad.drain()
    sum_hidden.drain()

    @pl.loop(0, items)
    def _(c):
        for way in range(2):
            hop = last - me if way == 0 else me
            onward = lax.rem(me + (tp - 1 if way == 0 else 1), tp)
            back = lax.rem(me + (1 if way == 0 else tp - 1), tp)

            @pl.when(hop < last)
            def _():
                rs_copy(way, c, onward).wait_send()

            @pl.when(hop > 0)
            def _():
                ag_copy(way, c, back).wait_send()

    for store in stores:
        store.wait()


def exchanged(x_teacher, x_student, t_gate, t_up, t_down, s_gate, s_up, s_down, align):
    tp, role = lax.axis_size("tp"), lax.axis_size("role")
    tokens, depth = x_teacher.shape
    half = tokens // 2
    units = t_gate.shape[1]
    chunk = width_of(units, 256)
    chunks = units // chunk
    items = GROUPS * chunks
    share = half // GROUPS
    wide, narrow, features = s_gate.shape[1], s_down.shape[1], align.shape[1]
    DMA = pltpu.SemaphoreType.DMA
    scratch = dict(
        sums=pltpu.VMEM((chunks, 2, half, 2 * chunk), F32),
        run=pltpu.VMEM((2, items, share, 2 * chunk), BF16),
        run_s=DMA((2, items)), run_r=DMA((2, items)),
        hid=pltpu.VMEM((items, 2, share, chunk), BF16),
        hid_s=DMA((2, items)), hid_r=DMA((2, items)),
        t_slot=pltpu.VMEM((TEACHER_SLOTS, depth, 2 * chunk), BF16),
        t_sem=DMA((TEACHER_SLOTS, 2)),
        d_slot=pltpu.VMEM((DOWN_SLOTS, chunk, features), BF16),
        d_sem=DMA((DOWN_SLOTS,)),
        w_gate=pltpu.VMEM(s_gate.shape, BF16),
        w_down=pltpu.VMEM(s_down.shape, BF16),
        w_align=pltpu.VMEM(align.shape, BF16),
        w_sem=DMA((4,)),
        gate_up=pltpu.VMEM((2, half, 2 * wide), F32),
        narrow=pltpu.VMEM((2, half, narrow), F32),
        diff=pltpu.VMEM((2, half, max(features, wide)), F32),
        so=pltpu.VMEM((2, half, narrow), BF16),
        ga=pltpu.VMEM((2, half, features), BF16),
        sh=pltpu.VMEM((2, half, wide), BF16),
        gso=pltpu.VMEM((2, half, narrow), BF16),
        gg=pltpu.VMEM((2, half, wide), BF16),
        gu=pltpu.VMEM((2, half, wide), BF16),
        o_sem=DMA((6,)),
        b_gate=sum_scratch(role, half, 2 * wide, BF16, 1),
        b_out=sum_scratch(tp, half, narrow, BF16, 1),
        b_diff=sum_scratch(role, half, features, BF16, 1),
        b_grad=sum_scratch(tp, half, narrow, BF16, 1),
        b_hidden=sum_scratch(role, half, wide, BF16, 2),
    )
    leaves, names = jax.tree.flatten(scratch, is_leaf=lambda leaf: not isinstance(leaf, dict))
    shapes = [narrow, features, wide, narrow, wide, wide]
    outs = pl.pallas_call(
        functools.partial(exchange_kernel, names, chunk),
        out_shape=[jax.ShapeDtypeStruct((2, half, n), BF16) for n in shapes],
        in_specs=[pl.BlockSpec(memory_space=pltpu.VMEM)] * 2 + [pl.BlockSpec(memory_space=pl.ANY)] * 7,
        out_specs=[pl.BlockSpec(memory_space=pl.ANY)] * 6,
        scratch_shapes=leaves,
        compiler_params=pltpu.CompilerParams(
            collective_id=0, has_side_effects=True, vmem_limit_bytes=60 * 2**20),
        cost_estimate=pl.CostEstimate(flops=20 * 10**9, bytes_accessed=70 * 10**6, transcendentals=10**6),
    )(x_teacher, x_student, t_gate, t_up, t_down, s_gate, s_up, s_down, align)
    return [out.reshape(tokens, out.shape[2]) for out in outs]


def outer_kernel(*refs):
    count = len(refs) // 3
    for i in range(count):
        refs[2 * count + i][...] = lax.dot_general(
            refs[i][...], refs[count + i][...], (((0,), (0,)), ((), ())),
            preferred_element_type=F32).astype(BF16)


def outer_products(lefts, rights):
    tokens = lefts[0].shape[0]
    steps = min(4, min(left.shape[1] for left in lefts) // 128)
    in_specs = [pl.BlockSpec((tokens, left.shape[1] // steps), lambda i: (0, i)) for left in lefts]
    in_specs += [pl.BlockSpec(right.shape, lambda i: (0, 0)) for right in rights]
    return pl.pallas_call(
        outer_kernel,
        grid=(steps,),
        out_shape=[jax.ShapeDtypeStruct((left.shape[1], right.shape[1]), BF16)
                   for left, right in zip(lefts, rights)],
        in_specs=in_specs,
        out_specs=[pl.BlockSpec((left.shape[1] // steps, right.shape[1]), lambda i: (i, 0))
                   for left, right in zip(lefts, rights)],
        compiler_params=pltpu.CompilerParams(vmem_limit_bytes=60 * 2**20),
    )(*lefts, *rights)


def on_device(x_teacher, x_student, *weights):
    student_out, grad_aligned, student_hidden, grad_student_out, grad_gate_pre, grad_up_pre = exchanged(
        x_teacher, x_student, *weights)
    return tuple(outer_products(
        [x_student, x_student, student_hidden, student_out],
        [grad_gate_pre, grad_up_pre, grad_student_out, grad_aligned]))


def solution(mesh):
    placed = (
        P("groups", "tp"),
        P("groups", "role"),
        P("tp", "role"),
        P("tp", "role"),
        P("role", "tp"),
        P("role", "tp"),
        P("role", "tp"),
        P("tp", "role"),
        P("role", "tp"),
    )
    return jax.shard_map(
        on_device,
        mesh=mesh,
        in_specs=placed,
        out_specs=(
            P(("groups", "role"), "tp"),
            P(("groups", "role"), "tp"),
            P(("groups", "tp"), "role"),
            P(("groups", "role"), "tp"),
        ),
        check_vma=False,
    )
```
